256 devices in a mesh: ctx: 64 (over z, x, core), head: 4 (over y).
Axes of the slice: x: 4, y: 4, z: 8, core: 2. Of those that a mesh axis runs over, the one named last changes fastest.
Arguments:
- queries: bfloat16 [16384, 4096], P('ctx', 'head'), may hold values from -6 to 6
- keys: bfloat16 [16384, 4096], P('ctx', 'head'), may hold values from -6 to 6
- values: bfloat16 [16384, 4096], P('ctx', 'head'), may hold values from -8 to 8
- out_grad: bfloat16 [16384, 4096], P('ctx', 'head'), may hold values from -8 to 8
- feature_weights: bfloat16 [128, 2, 32, 128], P('ctx', None, None, 'head'), may hold values from -0.5 to 0.5
Outputs:
- attended: bfloat16 [16384, 4096], P('ctx', 'head')
- query_grad: bfloat16 [16384, 4096], P('ctx', 'head')
- key_grad: bfloat16 [16384, 4096], P('ctx', 'head')
- value_grad: bfloat16 [16384, 4096], P('ctx', 'head')
- map_grad: float32 [128, 2, 32, 128], P('ctx', None, None, 'head')
The draws below stay inside these ranges and needn't reach their ends.
All inputs are finite; a program needn't handle non-finite values.
Results may differ from the reference program's by a relative error of at most 0.015.
Values may be sent and summed in bfloat16 or wider, within the bound.
No kernel may reach another device: no remote copies, remote signals or barrier semaphores. Data moves between devices by JAX's collectives and lax.ppermute only.
A program may use at most 192 MiB of HBM per device.

```python
import jax
import jax.numpy as jnp
from jax import lax

HEADS = 32
HEAD_DIM = 128
TOK_DEV = 256
TOKENS = 16384


def drifting(key):
    segment = TOK_DEV // 4
    segments = TOKENS // segment
    columns = HEADS * HEAD_DIM
    common = jax.random.normal(jax.random.fold_in(key, 1), (1, 1, columns), jnp.float32)
    drift = jax.random.normal(jax.random.fold_in(key, 2), (segments, 1, columns), jnp.float32)
    noise = jax.random.normal(jax.random.fold_in(key, 3), (segments, segment, columns), jnp.float32)
    whole = jnp.clip(common + drift + noise, -8.0, 8.0)
    return whole.reshape(TOKENS, columns).astype(jnp.bfloat16)


def rising_noise(key):
    segment = TOK_DEV // 4
    segments = TOKENS // segment
    columns = HEADS * HEAD_DIM
    noise = jax.random.normal(jax.random.fold_in(key, 3), (segments, segment, columns), jnp.float32)
    place = (jnp.arange(segments, dtype=jnp.float32) + 1.0) / segments
    ramp = 0.3 + 3.7 * place * place
    whole = jnp.clip(noise * ramp[:, None, None], -8.0, 8.0)
    return whole.reshape(TOKENS, columns).astype(jnp.bfloat16)


def draw_values(key, part):
    return drifting(jax.random.fold_in(key, 11))


def draw_out_grad(key, part):
    return rising_noise(jax.random.fold_in(key, 12))


def level_of(key, dims, split, low, high):
    factor_of, own = 1.0, jax.random.fold_in(key, 6)
    for position, shards_of in split:
        steps = jnp.exp(jax.random.uniform(jax.random.fold_in(own, position), (shards_of,), jnp.float32, low / len(split), high / len(split)))
        factor_of = factor_of * jnp.repeat(steps, dims[position] // shards_of).reshape([-1 if axis == position else 1 for axis in range(len(dims))])
    return factor_of


def normal_values(stream_key, extent, width, bound, pieces=(), held_as=jnp.bfloat16):
    array = jax.random.normal(stream_key, extent, jnp.float32) * width
    if len(pieces) > 0:
        array = level_of(stream_key, extent, pieces, -0.22, 0.18) * array
    return jnp.clip(array, min=-bound, max=bound).astype(held_as)


def setup_inputs(seed: int = 0) -> dict:
    streams_of = jax.random.split(jax.random.key(seed), 6)
    queries = normal_values(streams_of[0], (TOKENS, HEADS * HEAD_DIM), 1.0, 6.0, ((0, 64), (1, 4)))
    keys = normal_values(streams_of[1], (TOKENS, HEADS * HEAD_DIM), 1.0, 6.0, ((0, 64), (1, 4)))
    values = draw_values(jax.random.fold_in(streams_of[5], 71), 0)
    out_grad = draw_out_grad(jax.random.fold_in(streams_of[5], 71), 0)
    feature_weights = normal_values(streams_of[4], (HEAD_DIM, 2, HEADS, HEAD_DIM), HEAD_DIM ** -0.5, 0.5, ((0, 64), (3, 4)))
    return dict(queries=queries, keys=keys, values=values, out_grad=out_grad, feature_weights=feature_weights)


PRECISE = lax.Precision.HIGHEST


def elu_slope(pre_act):
    return jnp.where(pre_act > 0, 1.0, jnp.exp(jnp.minimum(pre_act, 0.0)))


def feature_pair(block_in, map_in):
    pre_act = jnp.einsum("tha,ahc->thc", block_in.astype(jnp.float32), map_in.astype(jnp.float32), precision=PRECISE)
    feats = (1.0 + jax.nn.elu(pre_act)).astype(jnp.bfloat16)
    return pre_act, feats


def causal_mask():
    row_ids = lax.broadcasted_iota(jnp.int32, (TOK_DEV, TOK_DEV), 0)
    col_ids = lax.broadcasted_iota(jnp.int32, (TOK_DEV, TOK_DEV), 1)
    return row_ids >= col_ids


def block_forward(query_blk, key_blk, value_blk, cot_blk, map_q, map_k, prior, prior_norm):
    pre_q, feat_q = feature_pair(query_blk, map_q)
    pre_k, feat_k = feature_pair(key_blk, map_k)
    fq_wide = feat_q.astype(jnp.float32)
    fk_wide = feat_k.astype(jnp.float32)
    causal = causal_mask()
    scores = jnp.einsum("thc,jhc->htj", fq_wide, fk_wide, precision=PRECISE)
    scores = jnp.where(causal[None], scores, 0.0)
    weights = scores.astype(jnp.bfloat16)
    numer = jnp.einsum("thc,hce->the", fq_wide, prior, precision=PRECISE)
    numer = numer + jnp.einsum("htj,jhe->the", weights.astype(jnp.float32), value_blk.astype(jnp.float32), precision=PRECISE)
    denom = jnp.einsum("thc,hc->th", fq_wide, prior_norm, precision=PRECISE) + jnp.sum(scores, axis=2).T
    attended_wide = numer / denom[:, :, None]
    grad = cot_blk.astype(jnp.float32) / denom[:, :, None]
    grad_half = grad.astype(jnp.bfloat16)
    slope_den = -jnp.sum(grad * attended_wide, axis=2)
    return pre_q, pre_k, feat_q, feat_k, weights, attended_wide, grad, grad_half, slope_den


def reference(queries, keys, values, out_grad, feature_weights):
    blocks = TOKENS // TOK_DEV
    shaped = (blocks, TOK_DEV, HEADS, HEAD_DIM)
    query_all = queries.reshape(shaped)
    key_all = keys.reshape(shaped)
    value_all = values.reshape(shaped)
    cot_all = out_grad.reshape(shaped)
    map_q = feature_weights[:, 0]
    map_k = feature_weights[:, 1]

    def first_pass(inputs):
        key_blk, value_blk = inputs
        pre_k, feat_k = feature_pair(key_blk, map_k)
        fk_wide = feat_k.astype(jnp.float32)
        state = jnp.einsum("thc,the->hce", fk_wide, value_blk.astype(jnp.float32), precision=PRECISE)
        return state, jnp.sum(fk_wide, axis=0)

    states, norms = lax.map(first_pass, (key_all, value_all))
    prior_all = jnp.concatenate([jnp.zeros_like(states[:1]), jnp.cumsum(states, axis=0)[:-1]], axis=0)
    prior_norm_all = jnp.concatenate([jnp.zeros_like(norms[:1]), jnp.cumsum(norms, axis=0)[:-1]], axis=0)

    def second_pass(inputs):
        query_blk, key_blk, value_blk, cot_blk, prior, prior_norm = inputs
        outs = block_forward(query_blk, key_blk, value_blk, cot_blk, map_q, map_k, prior, prior_norm)
        feat_q = outs[2]
        attended_wide = outs[5]
        grad = outs[6]
        slope_den = outs[8]
        fq_wide = feat_q.astype(jnp.float32)
        adjoint = jnp.einsum("thc,the->hce", fq_wide, grad, precision=PRECISE)
        adjoint_norm = jnp.einsum("th,thc->hc", slope_den, fq_wide, precision=PRECISE)
        return attended_wide.astype(jnp.bfloat16), adjoint, adjoint_norm

    attended, adjoints, adjoint_norms = lax.map(second_pass, (query_all, key_all, value_all, cot_all, prior_all, prior_norm_all))
    later_sum = jnp.cumsum(adjoints[::-1], axis=0)[::-1]
    later_norm = jnp.cumsum(adjoint_norms[::-1], axis=0)[::-1]
    after_all = jnp.concatenate([later_sum[1:], jnp.zeros_like(later_sum[:1])], axis=0)
    after_norm_all = jnp.concatenate([later_norm[1:], jnp.zeros_like(later_norm[:1])], axis=0)

    def third_pass(inputs):
        query_blk, key_blk, value_blk, cot_blk, prior, prior_norm, after, after_norm = inputs
        pre_q, pre_k, feat_q, feat_k, weights, attended_wide, grad, grad_half, slope_den = block_forward(
            query_blk, key_blk, value_blk, cot_blk, map_q, map_k, prior, prior_norm)
        fq_wide = feat_q.astype(jnp.float32)
        fk_wide = feat_k.astype(jnp.float32)
        value_wide = value_blk.astype(jnp.float32)
        causal = causal_mask()
        dscore = jnp.einsum("the,jhe->htj", grad_half.astype(jnp.float32), value_wide, precision=PRECISE) + slope_den.T[:, :, None]
        dscore = jnp.where(causal[None], dscore, 0.0).astype(jnp.bfloat16)
        dscore_wide = dscore.astype(jnp.float32)
        d_feat_q = jnp.einsum("hce,the->thc", prior, grad, precision=PRECISE)
        d_feat_q = d_feat_q + slope_den[:, :, None] * prior_norm[None]
        d_feat_q = d_feat_q + jnp.einsum("htj,jhc->thc", dscore_wide, fk_wide, precision=PRECISE)
        d_feat_k = jnp.einsum("hce,jhe->jhc", after, value_wide, precision=PRECISE) + after_norm[None]
        d_feat_k = d_feat_k + jnp.einsum("htj,thc->jhc", dscore_wide, fq_wide, precision=PRECISE)
        d_value = jnp.einsum("htj,the->jhe", weights.astype(jnp.float32), grad_half.astype(jnp.float32), precision=PRECISE)
        d_value = d_value + jnp.einsum("hce,jhc->jhe", after, fk_wide, precision=PRECISE)
        dpre_q = (d_feat_q * elu_slope(pre_q)).astype(jnp.bfloat16)
        dpre_k = (d_feat_k * elu_slope(pre_k)).astype(jnp.bfloat16)
        dpre_q_wide = dpre_q.astype(jnp.float32)
        dpre_k_wide = dpre_k.astype(jnp.float32)
        q_back = jnp.einsum("thc,ahc->tha", dpre_q_wide, map_q.astype(jnp.float32), precision=PRECISE).astype(jnp.bfloat16)
        k_back = jnp.einsum("thc,ahc->tha", dpre_k_wide, map_k.astype(jnp.float32), precision=PRECISE).astype(jnp.bfloat16)
        from_query = jnp.einsum("tha,thc->ahc", query_blk.astype(jnp.float32), dpre_q_wide, precision=PRECISE)
        from_key = jnp.einsum("tha,thc->ahc", key_blk.astype(jnp.float32), dpre_k_wide, precision=PRECISE)
        return q_back, k_back, d_value.astype(jnp.bfloat16), jnp.stack((from_query, from_key), axis=1)

    q_grads, k_grads, v_grads, terms = lax.map(third_pass, (query_all, key_all, value_all, cot_all, prior_all, prior_norm_all, after_all, after_norm_all))
    map_grad = jnp.sum(terms, axis=0) / TOKENS
    flat = (TOKENS, HEADS * HEAD_DIM)
    return attended.reshape(flat), q_grads.reshape(flat), k_grads.reshape(flat), v_grads.reshape(flat), map_grad
```

```python
import functools

import jax
import jax.numpy as jnp
from jax import lax
from jax.experimental import pallas as pl
from jax.experimental.pallas import tpu as pltpu
from jax.sharding import Mesh
from jax.sharding import PartitionSpec as P

HEAD_DIM = 128
BLOCK = 256
F32 = jnp.float32
BF16 = jnp.bfloat16
ROW = ("x", "core")
CTX = ("z", "x", "core")
EVERY = ("z", "x", "core", "y")


def mm(a, b):
    return lax.dot_general(a, b, (((1,), (0,)), ((), ())), preferred_element_type=F32)


def mm_nt(a, b):
    return lax.dot_general(a, b, (((1,), (1,)), ((), ())), preferred_element_type=F32)


def mm_tn(a, b):
    return lax.dot_general(a, b, (((0,), (0,)), ((), ())), preferred_element_type=F32)


def feature(pre):
    return jnp.where(pre > 0, pre + 1.0, jnp.exp(jnp.minimum(pre, 0.0)))


def halves(value):
    high = value.astype(BF16)
    return high, (value - high.astype(F32)).astype(BF16)


def causal_mask():
    rows = lax.broadcasted_iota(jnp.int32, (BLOCK, BLOCK), 0)
    cols = lax.broadcasted_iota(jnp.int32, (BLOCK, BLOCK), 1)
    return rows >= cols


def lanes(shape):
    return lax.broadcasted_iota(jnp.int32, shape, 1)


def row_slope(grad, attended):
    return jnp.broadcast_to(-jnp.sum(grad * attended, axis=1, keepdims=True), grad.shape)


def packed(total, out_ref):
    norms = total[:, HEAD_DIM:].T[:8]
    for z in range(out_ref.shape[0]):
        out_ref[z, :HEAD_DIM] = total[:, :HEAD_DIM]
        out_ref[z, HEAD_DIM:] = norms


def key_state(kv_ref, map_ref, fk_ref, out_ref):
    blocks = kv_ref.shape[0]
    ones = jnp.ones((BLOCK, HEAD_DIM), BF16)
    total = jnp.zeros((HEAD_DIM, 2 * HEAD_DIM), F32)
    for b in range(blocks):
        feat = feature(mm(kv_ref[b, 0], map_ref[...])).astype(BF16)
        fk_ref[b] = feat
        total = total + mm_tn(feat, jnp.concatenate([kv_ref[b, 1], ones], axis=1))
    packed(total, out_ref)


def forward(place_ref, kv_ref, qd_ref, fk_ref, map_ref, sums_ref,
            fq_ref, att_ref, weight_ref, grad_ref, slope_ref, high_ref, low_ref, adjoint_ref, out_ref):
    blocks = kv_ref.shape[0]
    place = place_ref[0]
    ones = jnp.ones((BLOCK, HEAD_DIM), BF16)
    prior = jnp.zeros((HEAD_DIM + 8, HEAD_DIM), F32)
    for z in range(sums_ref.shape[0]):
        prior = prior + jnp.where(z < place, sums_ref[z], 0.0)
    column = jnp.broadcast_to(prior[HEAD_DIM:HEAD_DIM + 1], (HEAD_DIM, HEAD_DIM)).T
    prior = jnp.concatenate([prior[:HEAD_DIM], column], axis=1)
    causal = causal_mask()
    lane = lanes((BLOCK, HEAD_DIM))
    total = jnp.zeros((HEAD_DIM, 2 * HEAD_DIM), F32)
    for b in range(blocks):
        feat_q = feature(mm(qd_ref[b, 0], map_ref[...])).astype(BF16)
        fq_ref[b] = feat_q
        feat_k = fk_ref[b]
        wide = jnp.concatenate([kv_ref[b, 1], ones], axis=1)
        high, low = halves(prior)
        high_ref[b] = high
        low_ref[b] = low
        scores = jnp.where(causal, mm_nt(feat_q, feat_k), 0.0)
        weight = scores.astype(BF16)
        weight_ref[b] = weight
        both = mm(jnp.concatenate([feat_q, feat_q], axis=1), jnp.concatenate([high, low], axis=0))
        inverse = 1.0 / (both[:, HEAD_DIM:] + jnp.sum(scores, axis=1, keepdims=True))
        attended = (both[:, :HEAD_DIM] + mm(weight, kv_ref[b, 1])) * inverse
        att_ref[b] = attended.astype(BF16)
        exact = qd_ref[b, 1].astype(F32) * inverse
        grad = exact.astype(BF16)
        slope_ref[b] = row_slope(exact, attended)
        slope_high, slope_low = halves(row_slope(grad.astype(F32), attended))
        none = jnp.zeros_like(slope_high)
        pair = jnp.where(lane == 0, slope_high, jnp.where(lane == 1, slope_low, none))
        grad = jnp.concatenate([grad, pair], axis=1)
        grad_ref[b] = grad
        adjoint = mm_tn(feat_q, grad)
        adjoint_ref[b] = adjoint
        total = total + adjoint
        prior = prior + mm_tn(feat_k, wide)
    packed(total, out_ref)


def query_side(kv_ref, qd_ref, fk_ref, fq_ref, att_ref, weight_ref, grad_ref, slope_ref, high_ref, low_ref, map_ref,
               aq_ref, key_ref, value_ref, map_grad_ref):
    blocks = kv_ref.shape[0]
    causal = causal_mask()
    map_grad = jnp.zeros((HEAD_DIM, HEAD_DIM), F32)
    for b in range(blocks):
        grad = grad_ref[b]
        half = grad[:, :HEAD_DIM]
        slope = slope_ref[b]
        feat_q = fq_ref[b]
        feat_k = fk_ref[b]
        dscore = mm_nt(half, kv_ref[b, 1]) + jnp.concatenate([slope, slope], axis=1)
        dscore = jnp.where(causal, dscore, 0.0).astype(BF16)
        d_feat = mm_nt(grad, high_ref[b]) + mm_nt(grad, low_ref[b]) + mm(dscore, feat_k)
        dpre = (d_feat * jnp.minimum(feat_q.astype(F32), 1.0)).astype(BF16)
        aq_ref[b, 0] = att_ref[b]
        aq_ref[b, 1] = mm_nt(dpre, map_ref[...]).astype(BF16)
        map_grad = map_grad + mm_tn(qd_ref[b, 0], dpre)
        key_ref[b] = mm_tn(dscore, feat_q)
        value_ref[b] = mm_tn(weight_ref[b], half)
    map_grad_ref[...] = map_grad


def key_side(place_ref, kv_ref, fk_ref, key_ref, value_ref, adjoint_ref, map_ref, sums_ref, out_ref, map_grad_ref):
    blocks = kv_ref.shape[0]
    place = place_ref[0]
    after = jnp.zeros((HEAD_DIM + 8, HEAD_DIM), F32)
    for z in range(sums_ref.shape[0]):
        after = after + jnp.where(z > place, sums_ref[z], 0.0)
    column = jnp.concatenate([after[HEAD_DIM:], jnp.zeros((HEAD_DIM - 8, HEAD_DIM), F32)], axis=0).T
    after = jnp.concatenate([after[:HEAD_DIM], column], axis=1)
    lane = lanes((BLOCK, HEAD_DIM))
    pair = jnp.where(lane < 2, 1.0, 0.0).astype(BF16)
    map_grad = jnp.zeros((HEAD_DIM, HEAD_DIM), F32)
    for b in range(blocks - 1, -1, -1):
        high, low = halves(after)
        feat_k = fk_ref[b]
        wide = jnp.concatenate([kv_ref[b, 1], pair], axis=1)
        d_feat = mm_nt(wide, high) + mm_nt(wide, low) + key_ref[b]
        dpre = (d_feat * jnp.minimum(feat_k.astype(F32), 1.0)).astype(BF16)
        out_ref[b, 0] = mm_nt(dpre, map_ref[...]).astype(BF16)
        stacked = jnp.concatenate([high[:, :HEAD_DIM], low[:, :HEAD_DIM]], axis=0)
        d_value = mm(jnp.concatenate([feat_k, feat_k], axis=1), stacked) + value_ref[b]
        out_ref[b, 1] = d_value.astype(BF16)
        map_grad = map_grad + mm_tn(kv_ref[b, 0], dpre)
        after = after + adjoint_ref[b]
    map_grad_ref[...] = map_grad


def call(kernel, shapes, scalars, flops, *operands):
    held = sum(v.size * v.dtype.itemsize for v in operands) + sum(
        s.size * s.dtype.itemsize for s in shapes
    )
    return pl.pallas_call(
        kernel,
        out_shape=shapes,
        in_specs=[pl.BlockSpec(memory_space=pltpu.SMEM)] * scalars
        + [pl.BlockSpec(memory_space=pltpu.VMEM)] * (len(operands) - scalars),
        out_specs=[pl.BlockSpec(memory_space=pltpu.VMEM)] * len(shapes),
        compiler_params=pltpu.CompilerParams(vmem_limit_bytes=40 * 1024 * 1024),
        cost_estimate=pl.CostEstimate(flops=flops, bytes_accessed=held, transcendentals=0),
    )(*operands)


def shape(*dims, dtype=BF16):
    return jax.ShapeDtypeStruct(dims, dtype)


def join_pair(first_ref, second_ref, out_ref):
    out_ref[0, 0] = first_ref[...]
    out_ref[0, 1] = second_ref[...]


def split_pair(in_ref, first_ref, second_ref):
    first_ref[...] = in_ref[0, 0]
    second_ref[...] = in_ref[0, 1]


def to_heads(first, second):
    rows, width = first.shape
    column = pl.BlockSpec((rows, HEAD_DIM), lambda h: (0, h))
    pieces = pl.pallas_call(
        join_pair,
        out_shape=shape(width // HEAD_DIM, 2, rows, HEAD_DIM),
        grid=(width // HEAD_DIM,),
        in_specs=[column, column],
        out_specs=pl.BlockSpec((1, 2, rows, HEAD_DIM), lambda h: (h, 0, 0, 0)),
    )(first, second)
    return lax.all_to_all(pieces, ROW, 0, 0, tiled=True)


def to_tokens(pieces):
    back = lax.all_to_all(pieces, ROW, 0, 0, tiled=True)
    heads, _, rows, _ = back.shape
    column = pl.BlockSpec((rows, HEAD_DIM), lambda h: (0, h))
    return pl.pallas_call(
        split_pair,
        out_shape=[shape(rows, heads * HEAD_DIM)] * 2,
        grid=(heads,),
        in_specs=[pl.BlockSpec((1, 2, rows, HEAD_DIM), lambda h: (h, 0, 0, 0))],
        out_specs=[column, column],
    )(back)


def body(queries, keys, values, out_grad, feature_weights):
    z_size, y_size = lax.axis_size("z"), lax.axis_size("y")
    row = lax.axis_size("x") * lax.axis_size("core")
    own, _, heads, cut = feature_weights.shape
    tokens = queries.shape[0] * lax.axis_size(CTX)
    place = lax.axis_index("z").astype(jnp.int32).reshape(1)

    kv = to_heads(keys, values)
    maps = feature_weights.transpose(2, 0, 1, 3).reshape(y_size, row, own * 2 * cut)
    maps = maps.transpose(1, 0, 2).reshape(1, heads, own * 2 * cut)
    maps = jnp.broadcast_to(maps, (z_size, heads, own * 2 * cut)).reshape(z_size * heads, -1)
    maps = lax.all_to_all(maps, EVERY, 0, 0, tiled=True)
    maps = maps.reshape(z_size * row, y_size, own, 2, cut).transpose(3, 0, 2, 1, 4)
    maps = maps.reshape(2, HEAD_DIM, HEAD_DIM)
    map_q, map_k = maps[0], maps[1]
    qd = to_heads(queries, out_grad)

    sums = shape(z_size, HEAD_DIM + 8, HEAD_DIM, dtype=F32)
    blocked = shape(row, BLOCK, HEAD_DIM)
    wide = shape(row, BLOCK, HEAD_DIM, dtype=F32)
    doubled = shape(row, BLOCK, 2 * HEAD_DIM)
    paired = shape(row, 2, BLOCK, HEAD_DIM)
    square = shape(HEAD_DIM, HEAD_DIM, dtype=F32)
    aug = shape(row, HEAD_DIM, 2 * HEAD_DIM)
    aug_wide = shape(row, HEAD_DIM, 2 * HEAD_DIM, dtype=F32)
    unit = 2 * row * BLOCK * HEAD_DIM * HEAD_DIM

    fk, state = call(key_state, [blocked, sums], 0, 3 * unit, kv, map_k)
    state = lax.all_to_all(state, "z", 0, 0, tiled=True)
    fq, att, weight, grad, slope, high, low, adjoint, total = call(
        forward,
        [blocked, blocked, doubled, doubled, wide, aug, aug, aug_wide, sums],
        1, 12 * unit, place, kv, qd, fk, map_q, state)
    total = lax.all_to_all(total, "z", 0, 0, tiled=True)
    aq, key_part, value_part, map_grad_q = call(
        query_side, [paired, wide, wide, square], 0, 14 * unit,
        kv, qd, fk, fq, att, weight, grad, slope, high, low, map_q)
    attended, query_grad = to_tokens(aq)
    dkv, map_grad_k = call(
        key_side, [paired, square], 1, 7 * unit,
        place, kv, fk, key_part, value_part, adjoint, map_k, total)
    key_grad, value_grad = to_tokens(dkv)

    map_grad = jnp.stack((map_grad_q, map_grad_k)).reshape(2, z_size * row, own, y_size, cut)
    map_grad = map_grad.transpose(1, 3, 2, 0, 4).reshape(z_size * heads, own * 2 * cut)
    map_grad = lax.all_to_all(map_grad, EVERY, 0, 0, tiled=True)
    map_grad = jnp.sum(map_grad.reshape(z_size, heads, own * 2 * cut), axis=0) / tokens
    map_grad = map_grad.reshape(row, y_size, own, 2, cut).transpose(2, 3, 1, 0, 4)
    map_grad = map_grad.reshape(own, 2, heads, cut)
    return attended, query_grad, key_grad, value_grad, map_grad


def solution(mesh):
    fine = Mesh(mesh.devices.reshape(8, 4, 2, 4), EVERY)
    flat = P(CTX, "y")
    maps = P(CTX, None, None, "y")
    return jax.shard_map(
        body,
        mesh=fine,
        in_specs=(flat, flat, flat, flat, maps),
        out_specs=(flat, flat, flat, flat, maps),
        check_vma=False,
    )
```

```python
import jax
import jax.numpy as jnp
from jax import lax
from jax.experimental import pallas as pl
from jax.experimental.pallas import tpu as pltpu
from jax.sharding import Mesh
from jax.sharding import PartitionSpec as P

HEAD_DIM = 128
BLOCK = 256
F32 = jnp.float32
BF16 = jnp.bfloat16
ROW = ("x", "core")
PLANE = ("z", "y")
CTX = ("z", "x", "core")
EVERY = ("z", "x", "core", "y")
HBM = pl.BlockSpec(memory_space=pltpu.HBM)
VMEM = pl.BlockSpec(memory_space=pltpu.VMEM)
SMEM = pl.BlockSpec(memory_space=pltpu.SMEM)
DMA = pltpu.SemaphoreType.DMA
AUX = 32
STATE_ROWS = HEAD_DIM + AUX


def mm(a, b):
    return lax.dot_general(a, b, (((1,), (0,)), ((), ())), preferred_element_type=F32)


def mm_nt(a, b):
    return lax.dot_general(a, b, (((1,), (1,)), ((), ())), preferred_element_type=F32)


def mm_tn(a, b):
    return lax.dot_general(a, b, (((0,), (0,)), ((), ())), preferred_element_type=F32)


def feature(pre):
    return jnp.where(pre > 0, pre + 1.0, jnp.exp(jnp.minimum(pre, 0.0)))


def halves(value):
    high = value.astype(BF16)
    return high, (value - high.astype(F32)).astype(BF16)


def causal_mask():
    rows = lax.broadcasted_iota(jnp.int32, (BLOCK, BLOCK), 0)
    cols = lax.broadcasted_iota(jnp.int32, (BLOCK, BLOCK), 1)
    return rows >= cols


def lanes(rows):
    return lax.broadcasted_iota(jnp.int32, (rows, HEAD_DIM), 1)


def row_slope(grad, attended):
    return jnp.broadcast_to(-jnp.sum(grad * attended, axis=1, keepdims=True), grad.shape)


def start_all(copies):
    for copy in copies:
        copy.start()
    return copies


def wait_all(copies):
    for copy in copies:
        copy.wait()


def norm_rows(column):
    rows = column.T[:16]
    index = lax.broadcasted_iota(jnp.int32, (16, HEAD_DIM), 0)
    high = rows.astype(BF16).astype(F32)
    mid = (rows - high).astype(BF16).astype(F32)
    low = rows - high - mid
    return jnp.where(
        index == 0, high, jnp.where(index == 1, mid, jnp.where(index == 2, low, 0.0))
    ).astype(BF16)


def pack_keys(k_ref, v_ref, map_ref, out_ref, sem):
    copies = []
    for h in range(out_ref.shape[0]):
        column = pl.ds(h * HEAD_DIM, HEAD_DIM)
        copies.append(pltpu.make_async_copy(k_ref.at[:, column], out_ref.at[h, pl.ds(0, BLOCK)], sem.at[h, 0]))
        copies.append(pltpu.make_async_copy(v_ref.at[:, column], out_ref.at[h, pl.ds(BLOCK, BLOCK)], sem.at[h, 1]))
        rows = pl.ds(h * AUX, AUX)
        copies.append(pltpu.make_async_copy(map_ref.at[rows], out_ref.at[h, pl.ds(2 * BLOCK, AUX)], sem.at[h, 2]))
    wait_all(start_all(copies))


def pack_pair(place_ref, first_ref, second_ref, *rest):
    outs, sem = rest[:-1], rest[-1]
    copies = []
    for s, out_ref in enumerate(outs):
        column = pl.ds(pl.multiple_of((place_ref[1] ^ s) * HEAD_DIM, HEAD_DIM), HEAD_DIM)
        copies.append(pltpu.make_async_copy(first_ref.at[:, column], out_ref.at[0], sem.at[s, 0]))
        copies.append(pltpu.make_async_copy(second_ref.at[:, column], out_ref.at[1], sem.at[s, 1]))
    wait_all(start_all(copies))


def split_pair(place_ref, *rest):
    pieces, (first_ref, second_ref, sem) = rest[:-3], rest[-3:]
    copies = []
    for s, in_ref in enumerate(pieces):
        column = pl.ds(pl.multiple_of((place_ref[1] ^ s) * HEAD_DIM, HEAD_DIM), HEAD_DIM)
        copies.append(pltpu.make_async_copy(in_ref.at[0], first_ref.at[:, column], sem.at[s, 0]))
        copies.append(pltpu.make_async_copy(in_ref.at[1], second_ref.at[:, column], sem.at[s, 1]))
    wait_all(start_all(copies))


def split_keys(in_ref, k_ref, v_ref, sem):
    copies = []
    for h in range(in_ref.shape[0]):
        column = pl.ds(h * HEAD_DIM, HEAD_DIM)
        copies.append(pltpu.make_async_copy(in_ref.at[h, pl.ds(0, BLOCK)], k_ref.at[:, column], sem.at[h, 0]))
        copies.append(pltpu.make_async_copy(in_ref.at[h, pl.ds(BLOCK, BLOCK)], v_ref.at[:, column], sem.at[h, 1]))
    wait_all(start_all(copies))


def key_state(kw_ref, map_ref, fk_ref, out_ref, kv, fk, send, in_sem, fk_sem, out_sem):
    blocks = kw_ref.shape[0]
    loads = start_all([
        pltpu.make_async_copy(kw_ref.at[b, pl.ds(0, 2 * BLOCK)], kv.at[b], in_sem.at[b]) for b in range(blocks)
    ])
    ones = jnp.ones((BLOCK, HEAD_DIM), BF16)
    total = jnp.zeros((HEAD_DIM, 2 * HEAD_DIM), F32)
    mean = jnp.zeros((1, HEAD_DIM), F32)
    stores = []
    for b in range(blocks):
        loads[b].wait()
        feat = feature(mm(kv[b, :BLOCK], map_ref[...])).astype(BF16)
        fk[b] = feat
        stores += start_all([pltpu.make_async_copy(fk.at[b], fk_ref.at[b], fk_sem.at[b])])
        value = kv[b, BLOCK:]
        mean = mean + jnp.sum(value.astype(F32), axis=0, keepdims=True)
        total = total + mm_tn(feat, jnp.concatenate([value, ones], axis=1))
    centre = (mean * (1.0 / (blocks * BLOCK))).astype(BF16)
    column = total[:, HEAD_DIM:]
    send[:HEAD_DIM] = (total[:, :HEAD_DIM] - column * centre.astype(F32)).astype(BF16)
    send[HEAD_DIM:HEAD_DIM + 16] = norm_rows(column)
    send[HEAD_DIM + 16:] = jnp.broadcast_to(centre, (16, HEAD_DIM))
    stores += start_all([
        pltpu.make_async_copy(send, out_ref.at[z], out_sem.at[z]) for z in range(out_ref.shape[0])
    ])
    wait_all(stores)


def forward(place_ref, kw_ref, fk_ref, map_ref, sums_ref, *rest):
    blocks = kw_ref.shape[0]
    qd_refs = rest[:blocks]
    (fq_ref, att_ref, weight_ref, grad_ref, high_ref, low_ref, adjoint_ref, out_ref,
     v, fk, qd, fq, att, weights, grads, highs, lows, adjoints, send,
     v_sem, fk_sem, qd_sem, store_sem, out_sem) = rest[blocks:]
    place = place_ref[0]
    loads = []
    for s in range(blocks):
        slot = place_ref[1] ^ s
        loads.append(pltpu.make_async_copy(qd_refs[s], qd.at[slot], qd_sem.at[s]))
        loads.append(pltpu.make_async_copy(kw_ref.at[s, pl.ds(BLOCK, BLOCK)], v.at[s], v_sem.at[s]))
        loads.append(pltpu.make_async_copy(fk_ref.at[s], fk.at[s], fk_sem.at[s]))
    start_all(loads)
    prior = jnp.zeros((HEAD_DIM, HEAD_DIM), F32)
    norms, centres = [], []
    for z in range(sums_ref.shape[0]):
        part = sums_ref[z].astype(F32)
        part = jnp.where(z < place, part, 0.0)
        prior = prior + part[:HEAD_DIM]
        norms.append(part[HEAD_DIM:HEAD_DIM + 16].astype(BF16))
        centres.append(sums_ref[z, HEAD_DIM + 16:])
    norms = jnp.concatenate(norms, axis=0)
    centres = jnp.concatenate(centres, axis=0)
    centres = jnp.concatenate([centres, jnp.ones_like(centres)], axis=1)
    prior = jnp.concatenate([prior, jnp.zeros_like(prior)], axis=1) + mm_tn(norms, centres)
    causal = causal_mask()
    lane = lanes(BLOCK)
    few = lanes(HEAD_DIM) < 2
    ones = jnp.ones((BLOCK, HEAD_DIM), BF16)
    total = jnp.zeros((HEAD_DIM, 2 * HEAD_DIM), F32)
    centre = jnp.zeros((1, HEAD_DIM), F32)
    wait_all(loads)
    stores = []
    for b in range(blocks):
        feat_q = feature(mm(qd[b, 0], map_ref[...])).astype(BF16)
        fq[b] = feat_q
        feat_k = fk[b]
        value = v[b]
        centre = centre + jnp.sum(value.astype(F32), axis=0, keepdims=True)
        high, low = halves(prior)
        none = jnp.zeros((HEAD_DIM, HEAD_DIM), BF16)
        highs[b] = jnp.concatenate([high[:, :HEAD_DIM], jnp.where(few, high[:, HEAD_DIM:], none)], axis=1)
        lows[b] = jnp.concatenate([low[:, :HEAD_DIM], jnp.where(few, low[:, HEAD_DIM:], none)], axis=1)
        scores = jnp.where(causal, mm_nt(feat_q, feat_k), 0.0)
        weight = scores.astype(BF16)
        weights[b] = weight
        both = mm(jnp.concatenate([feat_q, feat_q], axis=1), jnp.concatenate([high, low], axis=0))
        inverse = 1.0 / (both[:, HEAD_DIM:] + jnp.sum(scores, axis=1, keepdims=True))
        attended = (both[:, :HEAD_DIM] + mm(weight, value)) * inverse
        att[b] = attended.astype(BF16)
        exact = qd[b, 1].astype(F32) * inverse
        grad = exact.astype(BF16)
        within_high, within_low = halves(row_slope(exact, attended))
        across_high, across_low = halves(row_slope(grad.astype(F32), attended))
        pair = jnp.where(lane == 0, across_high, jnp.where(lane == 1, across_low, 0.0))
        pair = jnp.where(lane == 2, within_high, jnp.where(lane == 3, within_low, pair)).astype(BF16)
        grad = jnp.concatenate([grad, pair], axis=1)
        grads[b] = grad
        adjoint = mm_tn(feat_q, grad)
        adjoints[b] = adjoint
        total = total + adjoint
        prior = prior + mm_tn(feat_k, jnp.concatenate([value, ones], axis=1))
        pairs = ((fq, fq_ref), (att, att_ref), (weights, weight_ref), (grads, grad_ref),
                 (highs, high_ref), (lows, low_ref), (adjoints, adjoint_ref))
        stores += start_all([
            pltpu.make_async_copy(held.at[b], out.at[b], store_sem.at[n, b]) for n, (held, out) in enumerate(pairs)
        ])
    sent = total[:, :HEAD_DIM].astype(BF16)
    centre = (centre * (1.0 / (blocks * BLOCK))).astype(BF16).astype(F32)
    rest_of = jnp.sum((total[:, :HEAD_DIM] - sent.astype(F32)) * centre, axis=1, keepdims=True)
    column = jnp.sum(jnp.where(few, total[:, HEAD_DIM:], 0.0), axis=1, keepdims=True) + rest_of
    send[:HEAD_DIM] = sent
    send[HEAD_DIM:HEAD_DIM + 16] = norm_rows(jnp.broadcast_to(column, (HEAD_DIM, HEAD_DIM)))
    send[HEAD_DIM + 16:] = jnp.zeros((16, HEAD_DIM), BF16)
    stores += start_all([
        pltpu.make_async_copy(send, out_ref.at[z], out_sem.at[z]) for z in range(out_ref.shape[0])
    ])
    wait_all(stores)


def query_side(place_ref, kw_ref, fk_ref, map_ref, fq_ref, att_ref, weight_ref, grad_ref, high_ref, low_ref, *rest):
    blocks = kw_ref.shape[0]
    qd_refs, rest = rest[:blocks], rest[blocks:]
    aq_refs, rest = rest[:blocks], rest[blocks:]
    (key_ref, value_ref, map_grad_ref, v, q, fk, fq, weights, grads, highs, lows, dq, keys, values,
     att_sem, load_sem, q_sem, dq_sem, store_sem) = rest
    loads = [[] for _ in range(blocks)]
    others, turned = [], []
    for s in range(blocks):
        slot = place_ref[1] ^ s
        turned.append(pltpu.make_async_copy(qd_refs[s].at[0], q.at[slot], q_sem.at[s]))
        others.append(pltpu.make_async_copy(att_ref.at[slot], aq_refs[s].at[0], att_sem.at[s]))
    start_all(turned)
    for b in range(blocks):
        loads[b].append(pltpu.make_async_copy(kw_ref.at[b, pl.ds(BLOCK, BLOCK)], v.at[b], load_sem.at[0, b]))
        pairs = ((fk_ref, fk), (fq_ref, fq), (weight_ref, weights), (grad_ref, grads), (high_ref, highs), (low_ref, lows))
        for n, (held, into) in enumerate(pairs):
            loads[b].append(pltpu.make_async_copy(held.at[b], into.at[b], load_sem.at[n + 1, b]))
        start_all(loads[b])
    start_all(others)
    causal = causal_mask()
    lane = lanes(BLOCK)
    unit = jnp.where((lane == 2) | (lane == 3), 1.0, 0.0).astype(BF16)
    map_grad = jnp.zeros((HEAD_DIM, HEAD_DIM), F32)
    wait_all(turned)
    stores = []
    for b in range(blocks):
        wait_all(loads[b])
        grad = grads[b]
        feat_q = fq[b]
        dscore = mm_nt(grad, jnp.concatenate([v[b], unit], axis=1))
        dscore = jnp.where(causal, dscore, 0.0).astype(BF16)
        d_feat = mm_nt(grad, highs[b]) + mm_nt(grad, lows[b]) + mm(dscore, fk[b])
        dpre = (d_feat * jnp.minimum(feat_q.astype(F32), 1.0)).astype(BF16)
        dq[b] = mm_nt(dpre, map_ref[...]).astype(BF16)
        map_grad = map_grad + mm_tn(q[b], dpre)
        keys[b] = mm_tn(dscore, feat_q)
        values[b] = mm_tn(weights[b], grad[:, :HEAD_DIM])
        stores += start_all([
            pltpu.make_async_copy(keys.at[b], key_ref.at[b], store_sem.at[0, b]),
            pltpu.make_async_copy(values.at[b], value_ref.at[b], store_sem.at[1, b]),
        ])
    stores += start_all([
        pltpu.make_async_copy(dq.at[place_ref[1] ^ s], aq_refs[s].at[1], dq_sem.at[s]) for s in range(blocks)
    ])
    map_grad_ref[...] = map_grad
    wait_all(others)
    wait_all(stores)


def key_side(place_ref, kw_ref, fk_ref, key_ref, value_ref, adjoint_ref, map_ref, sums_ref, map_grad_ref,
             out_ref, kv, fk, keys, values, adjoints, out, load_sem, out_sem):
    blocks = kw_ref.shape[0]
    place = place_ref[0]
    loads = []
    for b in range(blocks):
        copies = [pltpu.make_async_copy(kw_ref.at[b, pl.ds(0, 2 * BLOCK)], kv.at[b], load_sem.at[0, b])]
        pairs = ((fk_ref, fk), (key_ref, keys), (value_ref, values), (adjoint_ref, adjoints))
        for n, (held, into) in enumerate(pairs):
            copies.append(pltpu.make_async_copy(held.at[b], into.at[b], load_sem.at[n + 1, b]))
        loads.append(copies)
    for b in range(blocks - 1, -1, -1):
        start_all(loads[b])
    after = jnp.zeros((HEAD_DIM, HEAD_DIM), F32)
    norms = []
    for z in range(sums_ref.shape[0]):
        part = jnp.where(z > place, sums_ref[z].astype(F32), 0.0)
        after = after + part[:HEAD_DIM]
        norms.append(part[HEAD_DIM:HEAD_DIM + 16].astype(BF16))
    norms = jnp.concatenate(norms, axis=0)
    first = jnp.where(lanes(HEAD_DIM) == 0, 1.0, 0.0).astype(BF16)
    after = jnp.concatenate([after, mm_tn(norms, first)], axis=1)
    pair = jnp.where(lanes(BLOCK) < 2, 1.0, 0.0).astype(BF16)
    map_grad = jnp.zeros((HEAD_DIM, HEAD_DIM), F32)
    for b in range(blocks - 1, -1, -1):
        wait_all(loads[b])
        high, low = halves(after)
        feat_k = fk[b]
        wide = jnp.concatenate([kv[b, BLOCK:], pair], axis=1)
        d_feat = mm_nt(wide, high) + mm_nt(wide, low) + keys[b]
        dpre = (d_feat * jnp.minimum(feat_k.astype(F32), 1.0)).astype(BF16)
        out[b, :BLOCK] = mm_nt(dpre, map_ref[...]).astype(BF16)
        stacked = jnp.concatenate([high[:, :HEAD_DIM], low[:, :HEAD_DIM]], axis=0)
        d_value = mm(jnp.concatenate([feat_k, feat_k], axis=1), stacked) + values[b]
        out[b, BLOCK:2 * BLOCK] = d_value.astype(BF16)
        map_grad = map_grad + mm_tn(kv[b, :BLOCK], dpre)
        after = after + adjoints[b]
    width = HEAD_DIM // blocks
    to = lax.broadcasted_iota(jnp.int32, (HEAD_DIM, HEAD_DIM), 0)
    of = lax.broadcasted_iota(jnp.int32, (HEAD_DIM, HEAD_DIM), 1)
    source = (to % width) // 2 * width + to // width * 2 + to % 2
    order = jnp.where(source == of, 1.0, 0.0).astype(BF16)
    for n, grad in enumerate((map_grad_ref[...], map_grad)):
        for m, part in enumerate(halves(grad)):
            rows = mm(order, part).astype(BF16)
            for b in range(blocks):
                at = 2 * BLOCK + (2 * n + m) * width
                out[b, at:at + width] = rows[b * width:(b + 1) * width]
    wait_all(start_all([
        pltpu.make_async_copy(out.at[b], out_ref.at[b], out_sem.at[b]) for b in range(blocks)
    ]))


def shape(*dims, dtype=BF16):
    return jax.ShapeDtypeStruct(dims, dtype)


def call(kernel, outs, operands, scratch, cycles=1, vmem=30):
    return pl.pallas_call(
        kernel,
        out_shape=[s for _, s in outs],
        in_specs=[spec for spec, _ in operands],
        out_specs=[spec for spec, _ in outs],
        scratch_shapes=scratch,
        compiler_params=pltpu.CompilerParams(vmem_limit_bytes=vmem * 1024 * 1024),
        cost_estimate=pl.CostEstimate(flops=cycles * 500_000_000, bytes_accessed=cycles * 2_000_000, transcendentals=0),
    )(*[v for _, v in operands])


def trade(pieces):
    count = len(pieces)
    return [pieces[0]] + [
        lax.ppermute(pieces[s], ROW, [(i, i ^ s) for i in range(count)]) for s in range(1, count)
    ]


def body(queries, keys, values, out_grad, feature_weights):
    z_size, y_size = lax.axis_size("z"), lax.axis_size("y")
    row = lax.axis_size("x") * lax.axis_size("core")
    own, _, heads, cut = feature_weights.shape
    tokens = queries.shape[0] * lax.axis_size(CTX)
    place = jnp.stack([lax.axis_index("z"), lax.axis_index(ROW)]).astype(jnp.int32)
    scratch = pltpu.VMEM

    maps = feature_weights.transpose(2, 0, 1, 3).reshape(1, heads, own * 2 * cut)
    maps = jnp.broadcast_to(maps, (z_size, heads, own * 2 * cut)).reshape(z_size * heads, -1)
    maps = lax.all_to_all(maps, PLANE, 0, 0, tiled=True)
    maps = maps.reshape(z_size * y_size, row, -1).transpose(1, 0, 2).reshape(row * AUX, HEAD_DIM)

    long = shape(row, 2 * BLOCK + AUX, HEAD_DIM)
    piece = shape(2, BLOCK, HEAD_DIM)
    (kw,) = call(pack_keys, [(HBM, long)], [(HBM, keys), (HBM, values), (HBM, maps)], [DMA((row, 3))])
    qd = call(pack_pair, [(HBM, piece)] * row, [(SMEM, place), (HBM, queries), (HBM, out_grad)], [DMA((row, 2))])
    kw = lax.all_to_all(kw, ROW, 0, 0, tiled=True)
    qd = trade(qd)
    maps = kw[:, 2 * BLOCK:].reshape(row, z_size, y_size, own, 2, cut).transpose(4, 1, 0, 3, 2, 5)
    maps = maps.reshape(2, HEAD_DIM, HEAD_DIM)
    map_q, map_k = maps[0], maps[1]

    sums = shape(z_size, STATE_ROWS, HEAD_DIM)
    one = (row, BLOCK, HEAD_DIM)
    two = (row, BLOCK, 2 * HEAD_DIM)
    aug = (row, HEAD_DIM, 2 * HEAD_DIM)
    send = scratch((STATE_ROWS, HEAD_DIM), BF16)

    fk, state = call(
        key_state, [(HBM, shape(*one)), (HBM, sums)], [(HBM, kw), (VMEM, map_k)],
        [scratch((row, 2 * BLOCK, HEAD_DIM), BF16), scratch(one, BF16), send, DMA((row,)), DMA((row,)), DMA((z_size,))])
    state = lax.all_to_all(state, "z", 0, 0, tiled=True)
    fq, att, weight, grad, high, low, adjoint, total = call(
        forward,
        [(HBM, shape(*one)), (HBM, shape(*one)), (HBM, shape(*two)), (HBM, shape(*two)), (HBM, shape(*aug)),
         (HBM, shape(*aug)), (HBM, shape(*aug, dtype=F32)), (HBM, sums)],
        [(SMEM, place), (HBM, kw), (HBM, fk), (VMEM, map_q), (VMEM, state)] + [(HBM, v) for v in qd],
        [scratch(one, BF16), scratch(one, BF16), scratch((row, 2, BLOCK, HEAD_DIM), BF16),
         scratch(one, BF16), scratch(one, BF16), scratch(two, BF16), scratch(two, BF16), scratch(aug, BF16),
         scratch(aug, BF16), scratch(aug, F32), send,
         DMA((row,)), DMA((row,)), DMA((row,)), DMA((7, row)), DMA((z_size,))], cycles=4)
    total = lax.all_to_all(total, "z", 0, 0, tiled=True)
    *aq, key_part, value_part, map_grad_q = call(
        query_side,
        [(HBM, piece)] * row + [(HBM, shape(*one, dtype=F32))] * 2 + [(VMEM, shape(HEAD_DIM, HEAD_DIM, dtype=F32))],
        [(SMEM, place), (HBM, kw), (HBM, fk), (VMEM, map_q), (HBM, fq), (HBM, att), (HBM, weight), (HBM, grad),
         (HBM, high), (HBM, low)] + [(HBM, v) for v in qd],
        [scratch(one, BF16), scratch(one, BF16), scratch(one, BF16), scratch(one, BF16), scratch(two, BF16),
         scratch(two, BF16), scratch(aug, BF16), scratch(aug, BF16), scratch(one, BF16), scratch(one, F32),
         scratch(one, F32), DMA((row,)), DMA((7, row)), DMA((row,)), DMA((row,)), DMA((2, row))], cycles=3)
    aq = trade(aq)
    flat = (HBM, shape(*queries.shape))
    width = 4 * HEAD_DIM // row
    longer = (row, 2 * BLOCK + width, HEAD_DIM)
    (dkv,) = call(
        key_side, [(HBM, shape(*longer))],
        [(SMEM, place), (HBM, kw), (HBM, fk), (HBM, key_part), (HBM, value_part), (HBM, adjoint), (VMEM, map_k),
         (VMEM, total), (VMEM, map_grad_q)],
        [scratch((row, 2 * BLOCK, HEAD_DIM), BF16), scratch(one, BF16), scratch(one, F32), scratch(one, F32),
         scratch(aug, F32), scratch(longer, BF16), DMA((5, row)), DMA((row,))], cycles=3)
    dkv = lax.all_to_all(dkv, ROW, 0, 0, tiled=True)
    attended, query_grad = call(
        split_pair, [flat, flat], [(SMEM, place)] + [(HBM, v) for v in aq], [DMA((row, 2))])
    key_grad, value_grad = call(split_keys, [flat, flat], [(HBM, dkv)], [DMA((row, 2))])

    map_grad = dkv[:, 2 * BLOCK:].reshape(row, 2, 2, z_size, own, y_size, cut).astype(F32)
    map_grad = map_grad[:, :, 0] + map_grad[:, :, 1]
    map_grad = map_grad.transpose(2, 4, 0, 1, 3, 5).reshape(z_size * heads, 2 * own * cut)
    map_grad = lax.all_to_all(map_grad, PLANE, 0, 0, tiled=True)
    map_grad = jnp.sum(map_grad.reshape(z_size, heads, 2, own, cut), axis=0) / tokens
    map_grad = map_grad.transpose(2, 1, 0, 3)
    return attended, query_grad, key_grad, value_grad, map_grad


def solution(mesh):
    fine = Mesh(mesh.devices.reshape(8, 4, 2, 4), EVERY)
    flat = P(CTX, "y")
    maps = P(CTX, None, None, "y")
    return jax.shard_map(
        body,
        mesh=fine,
        in_specs=(flat, flat, flat, flat, maps),
        out_specs=(flat, flat, flat, flat, maps),
        check_vma=False,
    )
```

```python
import jax
import jax.numpy as jnp
from jax import lax
from jax.experimental import pallas as pl
from jax.experimental.pallas import tpu as pltpu
from jax.sharding import Mesh
from jax.sharding import PartitionSpec as P

HEAD_DIM = 128
BLOCK = 256
F32 = jnp.float32
BF16 = jnp.bfloat16
ROW = ("x", "core")
CTX = ("z", "x", "core")
FINE = ("z", "x", "core", "y")
ANY = pl.BlockSpec(memory_space=pl.ANY)
VMEM = pl.BlockSpec(memory_space=pltpu.VMEM)
SMEM = pl.BlockSpec(memory_space=pltpu.SMEM)
DMA = pltpu.SemaphoreType.DMA
PART = BF16
STATE_ROWS = HEAD_DIM + 32


def mm(a, b):
    return lax.dot_general(a, b, (((1,), (0,)), ((), ())), preferred_element_type=F32)


def mm_nt(a, b):
    return lax.dot_general(a, b, (((1,), (1,)), ((), ())), preferred_element_type=F32)


def mm_tn(a, b):
    return lax.dot_general(a, b, (((0,), (0,)), ((), ())), preferred_element_type=F32)


def feature(pre):
    return jnp.where(pre > 0, pre + 1.0, jnp.exp(jnp.minimum(pre, 0.0)))


def halves(value):
    high = value.astype(BF16)
    return high, (value - high.astype(F32)).astype(BF16)


def causal_mask():
    rows = lax.broadcasted_iota(jnp.int32, (BLOCK, BLOCK), 0)
    cols = lax.broadcasted_iota(jnp.int32, (BLOCK, BLOCK), 1)
    return rows >= cols


def lanes(rows):
    return lax.broadcasted_iota(jnp.int32, (rows, HEAD_DIM), 1)


def row_slope(grad, attended):
    return jnp.broadcast_to(-jnp.sum(grad * attended, axis=1, keepdims=True), grad.shape)


def norm_rows(column):
    rows = column.T[:16]
    index = lax.broadcasted_iota(jnp.int32, (16, HEAD_DIM), 0)
    high = rows.astype(BF16).astype(F32)
    mid = (rows - high).astype(BF16).astype(F32)
    low = rows - high - mid
    return jnp.where(
        index == 0, high, jnp.where(index == 1, mid, jnp.where(index == 2, low, 0.0))
    ).astype(BF16)


def pack(place_ref, *refs):
    ins, outs, (held, in_sem, out_sem) = refs[:4], refs[4:-3], refs[-3:]
    loads, stores = [], []
    for s in range(len(outs)):
        column = pl.ds(pl.multiple_of((place_ref[1] ^ s) * HEAD_DIM, HEAD_DIM), HEAD_DIM)
        for n, ref in enumerate(ins):
            loads.append(pltpu.make_async_copy(ref.at[:, column], held.at[s, n], in_sem.at[s, n]))
        stores.append(pltpu.make_async_copy(held.at[s], outs[s], out_sem.at[s]))
    for load in loads:
        load.start()
    for s, store in enumerate(stores):
        for load in loads[4 * s:4 * s + 4]:
            load.wait()
        store.start()
    for store in stores:
        store.wait()


def unpack(place_ref, *refs):
    pieces, outs, sem = refs[:-3], refs[-3:-1], refs[-1]
    copies = []
    for s, piece in enumerate(pieces):
        column = pl.ds(pl.multiple_of((place_ref[1] ^ s) * HEAD_DIM, HEAD_DIM), HEAD_DIM)
        for n, ref in enumerate(outs):
            copies.append(pltpu.make_async_copy(piece.at[n], ref.at[:, column], sem.at[s, n]))
    for copy in copies:
        copy.start()
    for copy in copies:
        copy.wait()


def key_state(place_ref, map_ref, *refs):
    pieces, (kv_ref, qd_ref, out_ref) = refs[:-3], refs[-3:]
    blocks = len(pieces)
    for s, piece in enumerate(pieces):
        kv_ref[place_ref[1] ^ s] = piece[:2]
        qd_ref[place_ref[1] ^ s] = piece[2:]
    ones = jnp.ones((BLOCK, HEAD_DIM), BF16)
    total = jnp.zeros((HEAD_DIM, 2 * HEAD_DIM), F32)
    mean = jnp.zeros((1, HEAD_DIM), F32)
    for b in range(blocks):
        feat = feature(mm(kv_ref[b, 0], map_ref[1])).astype(BF16)
        value = kv_ref[b, 1]
        mean = mean + jnp.sum(value.astype(F32), axis=0, keepdims=True)
        total = total + mm_tn(feat, jnp.concatenate([value, ones], axis=1))
    centre = (mean * (1.0 / (blocks * BLOCK))).astype(BF16)
    column = total[:, HEAD_DIM:]
    state = (total[:, :HEAD_DIM] - column * centre.astype(F32)).astype(BF16)
    norms = norm_rows(column)
    for z in range(out_ref.shape[0]):
        out_ref[z, :HEAD_DIM] = state
        out_ref[z, HEAD_DIM:HEAD_DIM + 16] = norms
        out_ref[z, HEAD_DIM + 16:] = jnp.broadcast_to(centre, (16, HEAD_DIM))


def prior_of(place, sums_ref):
    prior = jnp.zeros((HEAD_DIM, HEAD_DIM), F32)
    norms, centres = [], []
    for z in range(sums_ref.shape[0]):
        part = jnp.where(z < place, sums_ref[z].astype(F32), 0.0)
        prior = prior + part[:HEAD_DIM]
        norms.append(part[HEAD_DIM:HEAD_DIM + 16].astype(BF16))
        centres.append(sums_ref[z, HEAD_DIM + 16:])
    centres = jnp.concatenate(centres, axis=0)
    centres = jnp.concatenate([centres, jnp.ones_like(centres)], axis=1)
    prior = jnp.concatenate([prior, jnp.zeros_like(prior)], axis=1)
    return prior + mm_tn(jnp.concatenate(norms, axis=0), centres)


def forward_block(kv_ref, qd_ref, b, map_ref, prior, causal):
    feat_k = feature(mm(kv_ref[b, 0], map_ref[1])).astype(BF16)
    feat_q = feature(mm(qd_ref[b, 0], map_ref[0])).astype(BF16)
    high, low = halves(prior)
    scores = jnp.where(causal, mm_nt(feat_q, feat_k), 0.0)
    weight = scores.astype(BF16)
    both = mm(jnp.concatenate([feat_q, feat_q], axis=1), jnp.concatenate([high, low], axis=0))
    inverse = 1.0 / (both[:, HEAD_DIM:] + jnp.sum(scores, axis=1, keepdims=True))
    attended = (both[:, :HEAD_DIM] + mm(weight, kv_ref[b, 1])) * inverse
    exact = qd_ref[b, 1].astype(F32) * inverse
    grad = exact.astype(BF16)
    across = halves(row_slope(grad.astype(F32), attended))
    return feat_k, feat_q, high, low, weight, attended, exact, grad, across


def with_ones(value):
    return jnp.concatenate([value, jnp.ones((BLOCK, HEAD_DIM), BF16)], axis=1)


def forward(place_ref, kv_ref, qd_ref, map_ref, sums_ref, out_ref):
    blocks = kv_ref.shape[0]
    prior = prior_of(place_ref[0], sums_ref)
    causal = causal_mask()
    lane = lanes(BLOCK)
    total = jnp.zeros((HEAD_DIM, 2 * HEAD_DIM), F32)
    centre = jnp.zeros((1, HEAD_DIM), F32)
    for b in range(blocks):
        feat_k, feat_q, _, _, _, _, _, grad, (across, rest) = forward_block(kv_ref, qd_ref, b, map_ref, prior, causal)
        pair = jnp.where(lane == 0, across, jnp.where(lane == 1, rest, jnp.zeros_like(rest)))
        total = total + mm_tn(feat_q, jnp.concatenate([grad, pair], axis=1))
        prior = prior + mm_tn(feat_k, with_ones(kv_ref[b, 1]))
        centre = centre + jnp.sum(kv_ref[b, 1].astype(F32), axis=0, keepdims=True)
    sent = total[:, :HEAD_DIM].astype(BF16)
    centre = (centre * (1.0 / (blocks * BLOCK))).astype(BF16).astype(F32)
    rest = jnp.sum((total[:, :HEAD_DIM] - sent.astype(F32)) * centre, axis=1, keepdims=True)
    column = jnp.sum(total[:, HEAD_DIM:], axis=1, keepdims=True) + rest
    norms = norm_rows(jnp.broadcast_to(column, (HEAD_DIM, HEAD_DIM)))
    for z in range(out_ref.shape[0]):
        out_ref[z, :HEAD_DIM] = sent
        out_ref[z, HEAD_DIM:HEAD_DIM + 16] = norms
        out_ref[z, HEAD_DIM + 16:] = jnp.zeros((16, HEAD_DIM), BF16)


def inner(place_ref, kv_ref, qd_ref, map_ref, sums_ref, *refs):
    pieces, (part_ref, map_grad_ref, aq, fqs, fks, grads, weights, dscores, adjoints) = refs[:-9], refs[-9:]
    blocks = kv_ref.shape[0]
    prior = prior_of(place_ref[0], sums_ref)
    causal = causal_mask()
    lane = lanes(BLOCK)
    few = lanes(HEAD_DIM) < 2
    unit = jnp.where((lane == 2) | (lane == 3), 1.0, 0.0).astype(BF16)
    none = jnp.zeros((HEAD_DIM, HEAD_DIM), BF16)
    map_grad = jnp.zeros((HEAD_DIM, HEAD_DIM), F32)
    for b in range(blocks):
        feat_k, feat_q, high, low, weight, attended, exact, half, (across, rest) = forward_block(
            kv_ref, qd_ref, b, map_ref, prior, causal)
        value = kv_ref[b, 1]
        within, within_rest = halves(row_slope(exact, attended))
        pair = jnp.where(lane == 0, across, jnp.where(lane == 1, rest, jnp.zeros_like(rest)))
        pair = jnp.where(lane == 2, within, jnp.where(lane == 3, within_rest, pair))
        grad = jnp.concatenate([half, pair], axis=1)
        fks[b] = feat_k
        fqs[b] = feat_q
        grads[b] = grad
        weights[b] = weight
        high = jnp.concatenate([high[:, :HEAD_DIM], jnp.where(few, high[:, HEAD_DIM:], none)], axis=1)
        low = jnp.concatenate([low[:, :HEAD_DIM], jnp.where(few, low[:, HEAD_DIM:], none)], axis=1)
        dscore = mm_nt(grad, jnp.concatenate([value, unit], axis=1))
        dscore = jnp.where(causal, dscore, 0.0).astype(BF16)
        dscores[b] = dscore
        d_feat = mm_nt(grad, high) + mm_nt(grad, low) + mm(dscore, feat_k)
        dpre = (d_feat * jnp.minimum(feat_q.astype(F32), 1.0)).astype(BF16)
        aq[b, 0] = attended.astype(BF16)
        aq[b, 1] = mm_nt(dpre, map_ref[0]).astype(BF16)
        map_grad = map_grad + mm_tn(qd_ref[b, 0], dpre)
        adjoints[b] = mm_tn(feat_q, grad)
        prior = prior + mm_tn(feat_k, with_ones(value))
    map_grad_ref[...] = map_grad
    for s, piece in enumerate(pieces):
        piece[...] = aq[place_ref[1] ^ s]
    pair = jnp.where(lane < 2, 1.0, 0.0).astype(BF16)
    after = jnp.zeros((HEAD_DIM, 2 * HEAD_DIM), F32)
    for b in range(blocks - 1, -1, -1):
        high, low = halves(after)
        wide = jnp.concatenate([kv_ref[b, 1], pair], axis=1)
        feat_k = fks[b]
        part_ref[b, 0] = (mm_nt(wide, high) + mm_nt(wide, low) + mm_tn(dscores[b], fqs[b])).astype(PART)
        stacked = jnp.concatenate([high[:, :HEAD_DIM], low[:, :HEAD_DIM]], axis=0)
        inside = mm_tn(weights[b], grads[b, :, :HEAD_DIM])
        part_ref[b, 1] = (mm(jnp.concatenate([feat_k, feat_k], axis=1), stacked) + inside).astype(PART)
        after = after + adjoints[b]


def outer(place_ref, kv_ref, map_ref, sums_ref, part_ref, out_ref, *pieces):
    place = place_ref[0]
    after = jnp.zeros((HEAD_DIM, HEAD_DIM), F32)
    norms = []
    for z in range(sums_ref.shape[0]):
        part = jnp.where(z > place, sums_ref[z].astype(F32), 0.0)
        after = after + part[:HEAD_DIM]
        norms.append(part[HEAD_DIM:HEAD_DIM + 16].astype(BF16))
    first = jnp.where(lanes(HEAD_DIM) == 0, 1.0, 0.0).astype(BF16)
    after = jnp.concatenate([after, mm_tn(jnp.concatenate(norms, axis=0), first)], axis=1)
    high, low = halves(after)
    stacked = jnp.concatenate([high[:, :HEAD_DIM], low[:, :HEAD_DIM]], axis=0)
    pair = jnp.where(lanes(BLOCK) == 0, 1.0, 0.0).astype(BF16)
    map_grad = jnp.zeros((HEAD_DIM, HEAD_DIM), F32)
    for s, piece in enumerate(pieces):
        b = place_ref[1] ^ s
        feat_k = feature(mm(kv_ref[b, 0], map_ref[1])).astype(BF16)
        wide = jnp.concatenate([kv_ref[b, 1], pair], axis=1)
        d_feat = mm_nt(wide, high) + mm_nt(wide, low) + part_ref[b, 0].astype(F32)
        dpre = (d_feat * jnp.minimum(feat_k.astype(F32), 1.0)).astype(BF16)
        d_value = mm(jnp.concatenate([feat_k, feat_k], axis=1), stacked) + part_ref[b, 1].astype(F32)
        piece[0] = mm_nt(dpre, map_ref[1]).astype(BF16)
        piece[1] = d_value.astype(BF16)
        map_grad = map_grad + mm_tn(kv_ref[b, 0], dpre)
    out_ref[...] = map_grad


def shape(*dims, dtype=BF16):
    return jax.ShapeDtypeStruct(dims, dtype)


def call(kernel, outs, operands, scratch=(), cycles=1, limit=32):
    return pl.pallas_call(
        kernel,
        out_shape=[s for _, s in outs],
        in_specs=[spec for spec, _ in operands],
        out_specs=[spec for spec, _ in outs],
        scratch_shapes=list(scratch),
        compiler_params=pltpu.CompilerParams(vmem_limit_bytes=limit * 1024 * 1024),
        cost_estimate=pl.CostEstimate(flops=cycles * 500_000_000, bytes_accessed=cycles * 2_000_000, transcendentals=0),
    )(*[v for _, v in operands])


def trade(pieces):
    count = len(pieces)
    return [pieces[0]] + [
        lax.ppermute(pieces[s], ROW, [(i, i ^ s) for i in range(count)]) for s in range(1, count)
    ]


def gather_maps(maps):
    z_size, y_size = lax.axis_size("z"), lax.axis_size("y")
    row = lax.axis_size(ROW)
    own, _, heads, cut = maps.shape
    maps = maps.transpose(2, 0, 1, 3).reshape(y_size, row, own * 2 * cut)
    maps = maps.transpose(1, 0, 2).reshape(1, heads, own * 2 * cut)
    return jnp.broadcast_to(maps, (z_size, heads, own * 2 * cut)).reshape(z_size * heads, -1)


def body(queries, keys, values, out_grad, feature_weights):
    z_size = lax.axis_size("z")
    row = lax.axis_size("x") * lax.axis_size("core")
    own, _, heads, cut = feature_weights.shape
    tokens = queries.shape[0] * lax.axis_size(CTX)
    place = jnp.stack([lax.axis_index("z"), lax.axis_index(ROW)]).astype(jnp.int32)
    scratch = pltpu.VMEM
    one = (row, BLOCK, HEAD_DIM)
    two = (row, BLOCK, 2 * HEAD_DIM)
    four = (4, BLOCK, HEAD_DIM)
    paired = (VMEM, shape(row, 2, BLOCK, HEAD_DIM))
    piece = (VMEM, shape(2, BLOCK, HEAD_DIM))
    sums = (VMEM, shape(z_size, STATE_ROWS, HEAD_DIM))
    square = (VMEM, shape(HEAD_DIM, HEAD_DIM, dtype=F32))

    pieces = call(
        pack, [(ANY, shape(*four))] * row, [(SMEM, place)] + [(ANY, v) for v in (keys, values, queries, out_grad)],
        [scratch((row, *four), BF16), DMA((row, 4)), DMA((row,))], limit=60)
    pieces = trade(pieces)
    maps = gather_maps(feature_weights)
    maps, pieces[1] = lax.optimization_barrier((maps, pieces[1]))
    maps = lax.all_to_all(maps, FINE, 0, 0, tiled=True)
    maps = maps.reshape(z_size * row, heads // row, own, 2, cut).transpose(3, 0, 2, 1, 4)
    maps = maps.reshape(2, HEAD_DIM, HEAD_DIM)
    kv, qd, state = call(
        key_state, [paired, paired, sums], [(SMEM, place), (VMEM, maps)] + [(VMEM, v) for v in pieces])
    state = lax.all_to_all(state, "z", 0, 0, tiled=True)
    held = [(SMEM, place), (VMEM, kv), (VMEM, qd), (VMEM, maps), (VMEM, state)]
    (total,) = call(forward, [sums], held, cycles=4)
    total = lax.all_to_all(total, "z", 0, 0, tiled=True)
    *aq, part, map_grad_q = call(
        inner,
        [piece] * row + [(VMEM, shape(row, 2, BLOCK, HEAD_DIM, dtype=PART)), square],
        held,
        [scratch((row, 2, BLOCK, HEAD_DIM), BF16), scratch(one, BF16), scratch(one, BF16), scratch(two, BF16),
         scratch(two, BF16), scratch(two, BF16), scratch((row, HEAD_DIM, 2 * HEAD_DIM), F32)], cycles=6)
    aq = trade(aq)
    map_grad_k, *dkv = call(
        outer, [square] + [piece] * row,
        [(SMEM, place), (VMEM, kv), (VMEM, maps), (VMEM, total), (VMEM, part)], cycles=3)
    dkv = trade(dkv)

    map_grad = jnp.stack((map_grad_q, map_grad_k)).reshape(2, z_size * row, own, heads // row, cut)
    map_grad = map_grad.transpose(1, 3, 2, 0, 4).reshape(z_size * heads, own * 2 * cut)
    map_grad, dkv[1] = lax.optimization_barrier((map_grad, dkv[1]))
    map_grad = lax.all_to_all(map_grad, FINE, 0, 0, tiled=True)
    map_grad = jnp.sum(map_grad.reshape(z_size, heads, own * 2 * cut), axis=0) / tokens
    map_grad = map_grad.reshape(row, heads // row, own, 2, cut).transpose(2, 3, 1, 0, 4)
    map_grad = map_grad.reshape(own, 2, heads, cut)
    outs = [(ANY, shape(*queries.shape))] * 2
    attended, query_grad = call(unpack, outs, [(SMEM, place)] + [(VMEM, v) for v in aq], [DMA((row, 2))])
    key_grad, value_grad = call(unpack, outs, [(SMEM, place)] + [(VMEM, v) for v in dkv], [DMA((row, 2))])
    return attended, query_grad, key_grad, value_grad, map_grad


def solution(mesh):
    fine = Mesh(mesh.devices.reshape(8, 4, 2, 4), FINE)
    flat = P(CTX, "y")
    maps = P(CTX, None, None, "y")
    return jax.shard_map(
        body,
        mesh=fine,
        in_specs=(flat, flat, flat, flat, maps),
        out_specs=(flat, flat, flat, flat, maps),
        check_vma=False,
    )
```

```python
import jax
import jax.numpy as jnp
from jax import lax
from jax.experimental import pallas as pl
from jax.experimental.pallas import tpu as pltpu
from jax.sharding import Mesh
from jax.sharding import PartitionSpec as P

HEAD_DIM = 128
BLOCK = 256
F32 = jnp.float32
BF16 = jnp.bfloat16
ROW = ("x", "core")
CTX = ("z", "x", "core")
FINE = ("z", "x", "core", "y")
ANY = pl.BlockSpec(memory_space=pl.ANY)
VMEM = pl.BlockSpec(memory_space=pltpu.VMEM)
SMEM = pl.BlockSpec(memory_space=pltpu.SMEM)
DMA = pltpu.SemaphoreType.DMA
PART = BF16
STATE_ROWS = HEAD_DIM + 16
GROUP = 4


def mm(a, b):
    return lax.dot_general(a, b, (((1,), (0,)), ((), ())), preferred_element_type=F32)


def mm_nt(a, b):
    return lax.dot_general(a, b, (((1,), (1,)), ((), ())), preferred_element_type=F32)


def mm_tn(a, b):
    return lax.dot_general(a, b, (((0,), (0,)), ((), ())), preferred_element_type=F32)


def feature(pre):
    return jnp.where(pre > 0, pre + 1.0, jnp.exp(jnp.minimum(pre, 0.0)))


def halves(value):
    high = value.astype(BF16)
    return high, (value - high.astype(F32)).astype(BF16)


def causal_mask():
    rows = lax.broadcasted_iota(jnp.int32, (BLOCK, BLOCK), 0)
    cols = lax.broadcasted_iota(jnp.int32, (BLOCK, BLOCK), 1)
    return rows >= cols


def lanes(rows):
    return lax.broadcasted_iota(jnp.int32, (rows, HEAD_DIM), 1)


def row_slope(grad, attended):
    return jnp.broadcast_to(-jnp.sum(grad * attended, axis=1, keepdims=True), grad.shape)


def norm_rows(column, centre):
    rows = column.T[:16]
    index = lax.broadcasted_iota(jnp.int32, (16, HEAD_DIM), 0)
    high = rows.astype(BF16).astype(F32)
    mid = (rows - high).astype(BF16).astype(F32)
    low = rows - high - mid
    parts = jnp.where(index == 0, high, jnp.where(index == 1, mid, jnp.where(index == 2, low, 0.0)))
    return jnp.where(index < 8, parts, jnp.broadcast_to(centre, (16, HEAD_DIM))).astype(BF16)


def turned(matrix):
    return matrix.astype(F32).T.astype(BF16)


def halves_into(value, high_ref, low_ref, b):
    high, low = halves(value)
    high_ref[b] = high
    low_ref[b] = low


def pack(place_ref, *refs):
    ins, outs, (held, in_sem, out_sem) = refs[:4], refs[4:-3], refs[-3:]
    loads, stores = [], []
    for s in range(len(outs)):
        column = pl.ds(pl.multiple_of((place_ref[1] ^ s) * HEAD_DIM, HEAD_DIM), HEAD_DIM)
        for n, ref in enumerate(ins):
            loads.append(pltpu.make_async_copy(ref.at[:, column], held.at[s, n], in_sem.at[s, n]))
        stores.append(pltpu.make_async_copy(held.at[s], outs[s], out_sem.at[s]))
    for load in loads:
        load.start()
    for s, store in enumerate(stores):
        for load in loads[4 * s:4 * s + 4]:
            load.wait()
        store.start()
    for store in stores:
        store.wait()


def unpack(place_ref, *refs):
    pieces, outs, sem = refs[:-5], refs[-5:-1], refs[-1]
    copies = []
    for s, piece in enumerate(pieces):
        column = pl.ds(pl.multiple_of((place_ref[1] ^ s) * HEAD_DIM, HEAD_DIM), HEAD_DIM)
        for n, ref in enumerate(outs):
            copies.append(pltpu.make_async_copy(piece.at[n], ref.at[:, column], sem.at[s, n]))
    for copy in copies:
        copy.start()
    for copy in copies:
        copy.wait()


def key_state(place_ref, map_ref, *refs):
    pieces, (kv_ref, qd_ref, out_ref) = refs[:-3], refs[-3:]
    blocks = len(pieces)
    for s, piece in enumerate(pieces):
        kv_ref[place_ref[1] ^ s] = piece[:2]
        qd_ref[place_ref[1] ^ s] = piece[2:]
    key_map = turned(map_ref[1])
    total = jnp.zeros((HEAD_DIM, 2 * HEAD_DIM), F32)
    mean = jnp.zeros((1, HEAD_DIM), F32)
    feats = [feature(mm_nt(key_map, kv_ref[b, 0])).astype(BF16) for b in range(blocks)]
    for b in range(blocks):
        value = kv_ref[b, 1]
        mean = mean + jnp.sum(value.astype(F32), axis=0, keepdims=True)
        total = total + mm(feats[b], with_ones(value))
    centre = (mean * (1.0 / (blocks * BLOCK))).astype(BF16).astype(F32)
    column = total[:, HEAD_DIM:]
    state = (total[:, :HEAD_DIM] - column * centre).astype(BF16)
    norms = norm_rows(column, centre)
    for z in range(out_ref.shape[0]):
        out_ref[z, :HEAD_DIM] = state
        out_ref[z, HEAD_DIM:] = norms


def with_ones(value):
    return jnp.concatenate([value, jnp.ones((BLOCK, HEAD_DIM), BF16)], axis=1)


def prior_of(place, sums_ref):
    prior = jnp.zeros((HEAD_DIM, HEAD_DIM), F32)
    norms, centres = [], []
    for z in range(sums_ref.shape[0]):
        part = jnp.where(z < place, sums_ref[z].astype(F32), 0.0)
        prior = prior + part[:HEAD_DIM]
        norms.append(part[HEAD_DIM:HEAD_DIM + 8])
        centres.append(part[HEAD_DIM + 8:])
    centres = jnp.concatenate(centres, axis=0).astype(BF16)
    centres = jnp.concatenate([centres, jnp.ones_like(centres)], axis=1)
    prior = jnp.concatenate([prior, jnp.zeros_like(prior)], axis=1)
    return prior + mm_tn(jnp.concatenate(norms, axis=0).astype(BF16), centres)


def key_stage(place, kv_ref, map_ref, sums_ref, highs, lows):
    blocks = kv_ref.shape[0]
    key_map = turned(map_ref[1])
    prior = prior_of(place, sums_ref)
    feats = [feature(mm_nt(key_map, kv_ref[b, 0])).astype(BF16) for b in range(blocks)]
    states = [mm(feats[b], with_ones(kv_ref[b, 1])) for b in range(blocks)]
    for b in range(blocks):
        halves_into(prior, highs, lows, b)
        prior = prior + states[b]
    return feats


def attend(group, kv_ref, qd_ref, feat_q, scores, highs, lows):
    weight = [s.astype(BF16) for s in scores]
    both = [mm(jnp.concatenate([f, f], axis=1), jnp.concatenate([highs[b], lows[b]], axis=0))
            for b, f in zip(group, feat_q)]
    inside = [mm(w, kv_ref[b, 1]) for b, w in zip(group, weight)]
    inverse = [1.0 / (p[:, HEAD_DIM:] + jnp.sum(s, axis=1, keepdims=True)) for p, s in zip(both, scores)]
    attended = [(p[:, :HEAD_DIM] + w) * i for p, w, i in zip(both, inside, inverse)]
    exact = [qd_ref[b, 1].astype(F32) * i for b, i in zip(group, inverse)]
    grad = [e.astype(BF16) for e in exact]
    across = [halves(row_slope(g.astype(F32), a)) for g, a in zip(grad, attended)]
    return attended, exact, grad, across


def groups_of(blocks):
    return [range(b, min(b + GROUP, blocks)) for b in range(0, blocks, GROUP)]


def forward(place_ref, kv_ref, qd_ref, map_ref, sums_ref, out_ref, highs, lows):
    blocks = kv_ref.shape[0]
    feats = key_stage(place_ref[0], kv_ref, map_ref, sums_ref, highs, lows)
    query_map = turned(map_ref[0])
    causal = causal_mask()
    lane = lanes(BLOCK)
    total = jnp.zeros((HEAD_DIM, 2 * HEAD_DIM), F32)
    centre = jnp.zeros((1, HEAD_DIM), F32)
    for group in groups_of(blocks):
        feat_q = [feature(mm(qd_ref[b, 0], map_ref[0])).astype(BF16) for b in group]
        feat_qt = [feature(mm_nt(query_map, qd_ref[b, 0])).astype(BF16) for b in group]
        scores = [jnp.where(causal, mm(f, feats[b]), 0.0) for b, f in zip(group, feat_q)]
        _, _, grads, across = attend(group, kv_ref, qd_ref, feat_q, scores, highs, lows)
        pairs = [jnp.where(lane == 0, a, jnp.where(lane == 1, r, jnp.zeros_like(r))) for a, r in across]
        for f, g, p in zip(feat_qt, grads, pairs):
            total = total + mm(f, jnp.concatenate([g, p], axis=1))
        for b in group:
            centre = centre + jnp.sum(kv_ref[b, 1].astype(F32), axis=0, keepdims=True)
    sent = total[:, :HEAD_DIM].astype(BF16)
    centre = (centre * (1.0 / (blocks * BLOCK))).astype(BF16).astype(F32)
    rest = jnp.sum((total[:, :HEAD_DIM] - sent.astype(F32)) * centre, axis=1, keepdims=True)
    column = jnp.sum(total[:, HEAD_DIM:], axis=1, keepdims=True) + rest
    norms = norm_rows(jnp.broadcast_to(column, (HEAD_DIM, HEAD_DIM)), jnp.zeros_like(centre))
    for z in range(out_ref.shape[0]):
        out_ref[z, :HEAD_DIM] = sent
        out_ref[z, HEAD_DIM:] = norms


def inner(place_ref, kv_ref, qd_ref, map_ref, sums_ref, aq_ref, part_ref, map_grad_ref,
          highs, lows, insides, adjoints, fks):
    blocks = kv_ref.shape[0]
    feats = key_stage(place_ref[0], kv_ref, map_ref, sums_ref, highs, lows)
    query_map = turned(map_ref[0])
    causal = causal_mask()
    rows = lax.broadcasted_iota(jnp.int32, (BLOCK, BLOCK), 0)
    cols = lax.broadcasted_iota(jnp.int32, (BLOCK, BLOCK), 1)
    anti = rows <= cols
    lane = lanes(BLOCK)
    few = lanes(HEAD_DIM) < 2
    unit = jnp.where((lane == 2) | (lane == 3), 1.0, 0.0).astype(BF16)
    none = jnp.zeros((HEAD_DIM, HEAD_DIM), BF16)
    map_grad = jnp.zeros((HEAD_DIM, HEAD_DIM), F32)

    def narrow(part):
        return jnp.concatenate([part[:, :HEAD_DIM], jnp.where(few, part[:, HEAD_DIM:], none)], axis=1)

    for group in groups_of(blocks):
        feat_q = [feature(mm(qd_ref[b, 0], map_ref[0])).astype(BF16) for b in group]
        feat_qt = [feature(mm_nt(query_map, qd_ref[b, 0])).astype(BF16) for b in group]
        feat_k = [feature(mm(kv_ref[b, 0], map_ref[1])).astype(BF16) for b in group]
        scores = [jnp.where(causal, mm(f, feats[b]), 0.0) for b, f in zip(group, feat_q)]
        weight_t = [jnp.where(anti, mm(k, q), 0.0).astype(BF16) for k, q in zip(feat_k, feat_qt)]
        attended, exact, halfs, across = attend(group, kv_ref, qd_ref, feat_q, scores, highs, lows)
        within = [halves(row_slope(e, a)) for e, a in zip(exact, attended)]
        pairs = [jnp.where(lane == 0, a, jnp.where(lane == 1, r, jnp.zeros_like(r))) for a, r in across]
        pairs = [jnp.where(lane == 2, a, jnp.where(lane == 3, r, p)) for p, (a, r) in zip(pairs, within)]
        grads = [jnp.concatenate([g, p], axis=1) for g, p in zip(halfs, pairs)]
        values = [jnp.concatenate([kv_ref[b, 1], unit], axis=1) for b in group]
        dscore = [jnp.where(causal, mm_nt(g, v), 0.0).astype(BF16) for g, v in zip(grads, values)]
        dscore_t = [jnp.where(anti, mm_nt(v, g), 0.0).astype(BF16) for g, v in zip(grads, values)]
        d_feat = [mm_nt(g, narrow(highs[b])) + mm_nt(g, narrow(lows[b])) + mm(d, k)
                  for b, g, d, k in zip(group, grads, dscore, feat_k)]
        dpre = [(d * jnp.minimum(f.astype(F32), 1.0)).astype(BF16) for d, f in zip(d_feat, feat_q)]
        for n, b in enumerate(group):
            aq_ref[b, 0] = attended[n].astype(BF16)
            aq_ref[b, 1] = mm_nt(dpre[n], map_ref[0]).astype(BF16)
            map_grad = map_grad + mm_tn(qd_ref[b, 0], dpre[n])
            insides[b, 0] = mm(dscore_t[n], feat_q[n])
            insides[b, 1] = mm(weight_t[n], halfs[n])
            adjoints[b] = mm(feat_qt[n], grads[n])
            fks[b] = feat_k[n]
    map_grad_ref[...] = map_grad
    pair = jnp.where(lane < 2, 1.0, 0.0).astype(BF16)
    after = jnp.zeros((HEAD_DIM, 2 * HEAD_DIM), F32)
    for b in range(blocks - 1, -1, -1):
        halves_into(after, highs, lows, b)
        after = after + adjoints[b]
    for b in range(blocks):
        wide = jnp.concatenate([kv_ref[b, 1], pair], axis=1)
        feat_k = fks[b]
        part_ref[b, 0] = (mm_nt(wide, highs[b]) + mm_nt(wide, lows[b]) + insides[b, 0]).astype(PART)
        stacked = jnp.concatenate([highs[b, :, :HEAD_DIM], lows[b, :, :HEAD_DIM]], axis=0)
        part_ref[b, 1] = (mm(jnp.concatenate([feat_k, feat_k], axis=1), stacked) + insides[b, 1]).astype(PART)


def outer(place_ref, kv_ref, map_ref, sums_ref, aq_ref, part_ref, out_ref, *pieces):
    place = place_ref[0]
    after = jnp.zeros((HEAD_DIM, HEAD_DIM), F32)
    norms = []
    for z in range(sums_ref.shape[0]):
        part = jnp.where(z > place, sums_ref[z].astype(F32), 0.0)
        after = after + part[:HEAD_DIM]
        norms.append(part[HEAD_DIM:HEAD_DIM + 8])
    norms = jnp.concatenate(norms, axis=0).astype(BF16)
    first = jnp.where(lax.broadcasted_iota(jnp.int32, norms.shape, 1) == 0, 1.0, 0.0).astype(BF16)
    after = jnp.concatenate([after, mm_tn(norms, first)], axis=1)
    high, low = halves(after)
    stacked = jnp.concatenate([high[:, :HEAD_DIM], low[:, :HEAD_DIM]], axis=0)
    pair = jnp.where(lanes(BLOCK) == 0, 1.0, 0.0).astype(BF16)
    map_grad = jnp.zeros((HEAD_DIM, HEAD_DIM), F32)
    for group in groups_of(len(pieces)):
        at = [place_ref[1] ^ s for s in group]
        feat_k = [feature(mm(kv_ref[b, 0], map_ref[1])).astype(BF16) for b in at]
        wide = [jnp.concatenate([kv_ref[b, 1], pair], axis=1) for b in at]
        d_feat = [mm_nt(w, high) + mm_nt(w, low) + part_ref[b, 0].astype(F32) for b, w in zip(at, wide)]
        dpre = [(d * jnp.minimum(f.astype(F32), 1.0)).astype(BF16) for d, f in zip(d_feat, feat_k)]
        d_value = [mm(jnp.concatenate([f, f], axis=1), stacked) + part_ref[b, 1].astype(F32)
                   for b, f in zip(at, feat_k)]
        for n, s in enumerate(group):
            pieces[s][:2] = aq_ref[at[n]]
            pieces[s][2] = mm_nt(dpre[n], map_ref[1]).astype(BF16)
            pieces[s][3] = d_value[n].astype(BF16)
            map_grad = map_grad + mm_tn(kv_ref[at[n], 0], dpre[n])
    out_ref[...] = map_grad


def shape(*dims, dtype=BF16):
    return jax.ShapeDtypeStruct(dims, dtype)


def call(kernel, outs, operands, scratch=(), cycles=1, limit=32):
    return pl.pallas_call(
        kernel,
        out_shape=[s for _, s in outs],
        in_specs=[spec for spec, _ in operands],
        out_specs=[spec for spec, _ in outs],
        scratch_shapes=list(scratch),
        compiler_params=pltpu.CompilerParams(vmem_limit_bytes=limit * 1024 * 1024),
        cost_estimate=pl.CostEstimate(flops=cycles * 500_000_000, bytes_accessed=cycles * 2_000_000, transcendentals=0),
    )(*[v for _, v in operands])


def trade(pieces):
    count = len(pieces)
    return [pieces[0]] + [
        lax.ppermute(pieces[s], ROW, [(i, i ^ s) for i in range(count)]) for s in range(1, count)
    ]


def gather_maps(maps):
    z_size, y_size = lax.axis_size("z"), lax.axis_size("y")
    row = lax.axis_size(ROW)
    own, _, heads, cut = maps.shape
    maps = maps.transpose(2, 0, 1, 3).reshape(y_size, row, own * 2 * cut)
    maps = maps.transpose(1, 0, 2).reshape(1, heads, own * 2 * cut)
    return jnp.broadcast_to(maps, (z_size, heads, own * 2 * cut)).reshape(z_size * heads, -1)


def body(queries, keys, values, out_grad, feature_weights):
    z_size = lax.axis_size("z")
    row = lax.axis_size("x") * lax.axis_size("core")
    own, _, heads, cut = feature_weights.shape
    tokens = queries.shape[0] * lax.axis_size(CTX)
    place = jnp.stack([lax.axis_index("z"), lax.axis_index(ROW)]).astype(jnp.int32)
    scratch = pltpu.VMEM
    four = (4, BLOCK, HEAD_DIM)
    paired = (VMEM, shape(row, 2, BLOCK, HEAD_DIM))
    sums = (VMEM, shape(z_size, STATE_ROWS, HEAD_DIM))
    square = (VMEM, shape(HEAD_DIM, HEAD_DIM, dtype=F32))

    pieces = call(
        pack, [(ANY, shape(*four))] * row, [(SMEM, place)] + [(ANY, v) for v in (keys, values, queries, out_grad)],
        [scratch((row, *four), BF16), DMA((row, 4)), DMA((row,))], limit=60)
    pieces = trade(pieces)
    maps = gather_maps(feature_weights)
    maps, pieces[1] = lax.optimization_barrier((maps, pieces[1]))
    maps = lax.all_to_all(maps, FINE, 0, 0, tiled=True)
    maps = maps.reshape(z_size * row, heads // row, own, 2, cut).transpose(3, 0, 2, 1, 4)
    maps = maps.reshape(2, HEAD_DIM, HEAD_DIM)
    kv, qd, state = call(
        key_state, [paired, paired, sums], [(SMEM, place), (VMEM, maps)] + [(VMEM, v) for v in pieces])
    state = lax.all_to_all(state, "z", 0, 0, tiled=True)
    held = [(SMEM, place), (VMEM, kv), (VMEM, qd), (VMEM, maps), (VMEM, state)]
    halved = [scratch((row, HEAD_DIM, 2 * HEAD_DIM), BF16)] * 2
    (total,) = call(forward, [sums], held, halved, cycles=4)
    total = lax.all_to_all(total, "z", 0, 0, tiled=True)
    aq, part, map_grad_q = call(
        inner, [paired, (VMEM, shape(row, 2, BLOCK, HEAD_DIM, dtype=PART)), square], held,
        halved + [scratch((row, 2, BLOCK, HEAD_DIM), F32), scratch((row, HEAD_DIM, 2 * HEAD_DIM), F32),
                  scratch((row, BLOCK, HEAD_DIM), BF16)], cycles=6)
    map_grad_k, *pieces = call(
        outer, [square] + [(VMEM, shape(*four))] * row,
        [(SMEM, place), (VMEM, kv), (VMEM, maps), (VMEM, total), (VMEM, aq), (VMEM, part)], cycles=3)
    pieces = trade(pieces)

    map_grad = jnp.stack((map_grad_q, map_grad_k)).reshape(2, z_size * row, own, heads // row, cut)
    map_grad = map_grad.transpose(1, 3, 2, 0, 4).reshape(z_size * heads, own * 2 * cut)
    map_grad, pieces[1] = lax.optimization_barrier((map_grad, pieces[1]))
    map_grad = lax.all_to_all(map_grad, FINE, 0, 0, tiled=True)
    map_grad = jnp.sum(map_grad.reshape(z_size, heads, own * 2 * cut), axis=0) / tokens
    map_grad = map_grad.reshape(row, heads // row, own, 2, cut).transpose(2, 3, 1, 0, 4)
    map_grad = map_grad.reshape(own, 2, heads, cut)
    attended, query_grad, key_grad, value_grad = call(
        unpack, [(ANY, shape(*queries.shape))] * 4, [(SMEM, place)] + [(VMEM, v) for v in pieces], [DMA((row, 4))])
    return attended, query_grad, key_grad, value_grad, map_grad


def solution(mesh):
    fine = Mesh(mesh.devices.reshape(8, 4, 2, 4), FINE)
    flat = P(CTX, "y")
    maps = P(CTX, None, None, "y")
    return jax.shard_map(
        body,
        mesh=fine,
        in_specs=(flat, flat, flat, flat, maps),
        out_specs=(flat, flat, flat, flat, maps),
        check_vma=False,
    )
```

```python
import jax
import jax.numpy as jnp
from jax import lax
from jax.experimental import pallas as pl
from jax.experimental.pallas import tpu as pltpu
from jax.sharding import Mesh
from jax.sharding import PartitionSpec as P

HEAD_DIM = 128
BLOCK = 256
F32 = jnp.float32
BF16 = jnp.bfloat16
ROW = ("x", "core")
CTX = ("z", "x", "core")
FINE = ("z", "x", "core", "y")
ANY = pl.BlockSpec(memory_space=pl.ANY)
VMEM = pl.BlockSpec(memory_space=pltpu.VMEM)
SMEM = pl.BlockSpec(memory_space=pltpu.SMEM)
DMA = pltpu.SemaphoreType.DMA
PART = BF16
STATE_ROWS = HEAD_DIM + 16
GROUP = 4
OUTER_LIMIT = 32
HELD = 40


def mm(a, b):
    return lax.dot_general(a, b, (((1,), (0,)), ((), ())), preferred_element_type=F32)


def mm_nt(a, b):
    return lax.dot_general(a, b, (((1,), (1,)), ((), ())), preferred_element_type=F32)


def mm_tn(a, b):
    return lax.dot_general(a, b, (((0,), (0,)), ((), ())), preferred_element_type=F32)


def feature(pre):
    return jnp.where(pre > 0, pre + 1.0, jnp.exp(jnp.minimum(pre, 0.0)))


def halves(value):
    high = value.astype(BF16)
    return high, (value - high.astype(F32)).astype(BF16)


def causal_mask():
    rows = lax.broadcasted_iota(jnp.int32, (BLOCK, BLOCK), 0)
    cols = lax.broadcasted_iota(jnp.int32, (BLOCK, BLOCK), 1)
    return rows >= cols


def lanes(rows):
    return lax.broadcasted_iota(jnp.int32, (rows, HEAD_DIM), 1)


def row_slope(grad, attended):
    return jnp.broadcast_to(-jnp.sum(grad * attended, axis=1, keepdims=True), grad.shape)


def norm_rows(column, centre):
    rows = column.T[:16]
    index = lax.broadcasted_iota(jnp.int32, (16, HEAD_DIM), 0)
    high = rows.astype(BF16).astype(F32)
    mid = (rows - high).astype(BF16).astype(F32)
    low = rows - high - mid
    parts = jnp.where(index == 0, high, jnp.where(index == 1, mid, jnp.where(index == 2, low, 0.0)))
    return jnp.where(index < 8, parts, jnp.broadcast_to(centre, (16, HEAD_DIM))).astype(BF16)


def turned(matrix):
    return matrix.astype(F32).T.astype(BF16)


def halves_into(value, high_ref, low_ref, b):
    high, low = halves(value)
    high_ref[b] = high
    low_ref[b] = low


def pack(*refs):
    me = lax.axis_index(ROW)
    ins, outs, (held, in_sem, out_sem) = refs[:4], refs[4:-3], refs[-3:]
    loads, stores = [], []
    for s in range(len(outs)):
        column = pl.ds(pl.multiple_of((me ^ s) * HEAD_DIM, HEAD_DIM), HEAD_DIM)
        for n, ref in enumerate(ins):
            loads.append(pltpu.make_async_copy(ref.at[:, column], held.at[s, n], in_sem.at[s, n]))
        stores.append(pltpu.make_async_copy(held.at[s], outs[s], out_sem.at[s]))
    for load in loads:
        load.start()
    for s, store in enumerate(stores):
        for load in loads[4 * s:4 * s + 4]:
            load.wait()
        store.start()
    for store in stores:
        store.wait()


def unpack(place_ref, *refs):
    pieces, outs, sem = refs[:-5], refs[-5:-1], refs[-1]
    copies = []
    for s, piece in enumerate(pieces):
        column = pl.ds(pl.multiple_of((place_ref[1] ^ s) * HEAD_DIM, HEAD_DIM), HEAD_DIM)
        for n, ref in enumerate(outs):
            copies.append(pltpu.make_async_copy(piece.at[n], ref.at[:, column], sem.at[s, n]))
    for copy in copies:
        copy.start()
    for copy in copies:
        copy.wait()


def key_state(place_ref, map_ref, *refs):
    pieces, (kv_ref, qd_ref, out_ref) = refs[:-3], refs[-3:]
    blocks = len(pieces)
    me = place_ref[1]
    for s, piece in enumerate(pieces):
        kv_ref[me ^ s] = piece[:2]
        qd_ref[me ^ s] = piece[2:]
    key_map = turned(map_ref[1])
    total = jnp.zeros((HEAD_DIM, 2 * HEAD_DIM), F32)
    mean = jnp.zeros((1, HEAD_DIM), F32)
    feats = [feature(mm_nt(key_map, piece[0])).astype(BF16) for piece in pieces]
    for feat, piece in zip(feats, pieces):
        value = piece[1]
        mean = mean + jnp.sum(value.astype(F32), axis=0, keepdims=True)
        total = total + mm(feat, with_ones(value))
    centre = (mean * (1.0 / (blocks * BLOCK))).astype(BF16).astype(F32)
    column = total[:, HEAD_DIM:]
    state = (total[:, :HEAD_DIM] - column * centre).astype(BF16)
    norms = norm_rows(column, centre)
    for z in range(out_ref.shape[0]):
        out_ref[z, :HEAD_DIM] = state
        out_ref[z, HEAD_DIM:] = norms


def with_ones(value):
    return jnp.concatenate([value, jnp.ones((BLOCK, HEAD_DIM), BF16)], axis=1)


def prior_of(place, sums_ref):
    prior = jnp.zeros((HEAD_DIM, HEAD_DIM), F32)
    norms, centres = [], []
    for z in range(sums_ref.shape[0]):
        part = jnp.where(z < place, sums_ref[z].astype(F32), 0.0)
        prior = prior + part[:HEAD_DIM]
        norms.append(part[HEAD_DIM:HEAD_DIM + 8])
        centres.append(part[HEAD_DIM + 8:])
    centres = jnp.concatenate(centres, axis=0).astype(BF16)
    centres = jnp.concatenate([centres, jnp.ones_like(centres)], axis=1)
    prior = jnp.concatenate([prior, jnp.zeros_like(prior)], axis=1)
    return prior + mm_tn(jnp.concatenate(norms, axis=0).astype(BF16), centres)


def key_stage(prior, kv_ref, map_ref, highs, lows):
    blocks = kv_ref.shape[0]
    key_map = turned(map_ref[1])
    feats = [feature(mm_nt(key_map, kv_ref[b, 0])).astype(BF16) for b in range(blocks)]
    states = [mm(feats[b], with_ones(kv_ref[b, 1])) for b in range(blocks)]
    for b in range(blocks):
        halves_into(prior, highs, lows, b)
        prior = prior + states[b]
    return feats


def attend(group, kv_ref, qd_ref, feat_q, scores, highs, lows):
    weight = [s.astype(BF16) for s in scores]
    both = [mm(jnp.concatenate([f, f], axis=1), jnp.concatenate([highs[b], lows[b]], axis=0))
            for b, f in zip(group, feat_q)]
    inside = [mm(w, kv_ref[b, 1]) for b, w in zip(group, weight)]
    inverse = [1.0 / (p[:, HEAD_DIM:] + jnp.sum(s, axis=1, keepdims=True)) for p, s in zip(both, scores)]
    attended = [(p[:, :HEAD_DIM] + w) * i for p, w, i in zip(both, inside, inverse)]
    exact = [qd_ref[b, 1].astype(F32) * i for b, i in zip(group, inverse)]
    grad = [e.astype(BF16) for e in exact]
    across = [halves(row_slope(g.astype(F32), a)) for g, a in zip(grad, attended)]
    return attended, exact, grad, across


def groups_of(blocks):
    return [range(b, min(b + GROUP, blocks)) for b in range(0, blocks, GROUP)]


def forward(place_ref, kv_ref, qd_ref, map_ref, sums_ref, out_ref, prior_ref, highs, lows):
    blocks = kv_ref.shape[0]
    prior = prior_of(place_ref[0], sums_ref)
    prior_ref[...] = prior
    feats = key_stage(prior, kv_ref, map_ref, highs, lows)
    query_map = turned(map_ref[0])
    causal = causal_mask()
    lane = lanes(BLOCK)
    total = jnp.zeros((HEAD_DIM, 2 * HEAD_DIM), F32)
    centre = jnp.zeros((1, HEAD_DIM), F32)
    for group in groups_of(blocks):
        feat_q = [feature(mm(qd_ref[b, 0], map_ref[0])).astype(BF16) for b in group]
        feat_qt = [feature(mm_nt(query_map, qd_ref[b, 0])).astype(BF16) for b in group]
        scores = [jnp.where(causal, mm(f, feats[b]), 0.0) for b, f in zip(group, feat_q)]
        _, _, grads, across = attend(group, kv_ref, qd_ref, feat_q, scores, highs, lows)
        pairs = [jnp.where(lane == 0, a, jnp.where(lane == 1, r, jnp.zeros_like(r))) for a, r in across]
        for f, g, p in zip(feat_qt, grads, pairs):
            total = total + mm(f, jnp.concatenate([g, p], axis=1))
        for b in group:
            centre = centre + jnp.sum(kv_ref[b, 1].astype(F32), axis=0, keepdims=True)
    sent = total[:, :HEAD_DIM].astype(BF16)
    centre = (centre * (1.0 / (blocks * BLOCK))).astype(BF16).astype(F32)
    rest = jnp.sum((total[:, :HEAD_DIM] - sent.astype(F32)) * centre, axis=1, keepdims=True)
    column = jnp.sum(total[:, HEAD_DIM:], axis=1, keepdims=True) + rest
    norms = norm_rows(jnp.broadcast_to(column, (HEAD_DIM, HEAD_DIM)), jnp.zeros_like(centre))
    for z in range(out_ref.shape[0]):
        out_ref[z, :HEAD_DIM] = sent
        out_ref[z, HEAD_DIM:] = norms


def inner(kv_ref, qd_ref, map_ref, prior_ref, aq_ref, part_ref, map_grad_ref,
          highs, lows, insides, adjoints, fks, aq, sem):
    blocks = kv_ref.shape[0]
    feats = key_stage(prior_ref[...], kv_ref, map_ref, highs, lows)
    stores = [pltpu.make_async_copy(aq.at[b], aq_ref.at[0, b], sem.at[b]) for b in range(blocks)]
    query_map = turned(map_ref[0])
    causal = causal_mask()
    rows = lax.broadcasted_iota(jnp.int32, (BLOCK, BLOCK), 0)
    cols = lax.broadcasted_iota(jnp.int32, (BLOCK, BLOCK), 1)
    anti = rows <= cols
    lane = lanes(BLOCK)
    few = lanes(HEAD_DIM) < 2
    unit = jnp.where((lane == 2) | (lane == 3), 1.0, 0.0).astype(BF16)
    none = jnp.zeros((HEAD_DIM, HEAD_DIM), BF16)
    map_grad = jnp.zeros((HEAD_DIM, HEAD_DIM), F32)

    def narrow(part):
        return jnp.concatenate([part[:, :HEAD_DIM], jnp.where(few, part[:, HEAD_DIM:], none)], axis=1)

    for group in groups_of(blocks):
        feat_q = [feature(mm(qd_ref[b, 0], map_ref[0])).astype(BF16) for b in group]
        feat_qt = [feature(mm_nt(query_map, qd_ref[b, 0])).astype(BF16) for b in group]
        feat_k = [feature(mm(kv_ref[b, 0], map_ref[1])).astype(BF16) for b in group]
        scores = [jnp.where(causal, mm(f, feats[b]), 0.0) for b, f in zip(group, feat_q)]
        weight_t = [jnp.where(anti, mm(k, q), 0.0).astype(BF16) for k, q in zip(feat_k, feat_qt)]
        attended, exact, halfs, across = attend(group, kv_ref, qd_ref, feat_q, scores, highs, lows)
        within = [halves(row_slope(e, a)) for e, a in zip(exact, attended)]
        pairs = [jnp.where(lane == 0, a, jnp.where(lane == 1, r, jnp.zeros_like(r))) for a, r in across]
        pairs = [jnp.where(lane == 2, a, jnp.where(lane == 3, r, p)) for p, (a, r) in zip(pairs, within)]
        grads = [jnp.concatenate([g, p], axis=1) for g, p in zip(halfs, pairs)]
        values = [jnp.concatenate([kv_ref[b, 1], unit], axis=1) for b in group]
        dscore = [jnp.where(causal, mm_nt(g, v), 0.0).astype(BF16) for g, v in zip(grads, values)]
        dscore_t = [jnp.where(anti, mm_nt(v, g), 0.0).astype(BF16) for g, v in zip(grads, values)]
        d_feat = [mm_nt(g, narrow(highs[b])) + mm_nt(g, narrow(lows[b])) + mm(d, k)
                  for b, g, d, k in zip(group, grads, dscore, feat_k)]
        dpre = [(d * jnp.minimum(f.astype(F32), 1.0)).astype(BF16) for d, f in zip(d_feat, feat_q)]
        for n, b in enumerate(group):
            aq[b, 0] = attended[n].astype(BF16)
            aq[b, 1] = mm_nt(dpre[n], map_ref[0]).astype(BF16)
            stores[b].start()
            map_grad = map_grad + mm_tn(qd_ref[b, 0], dpre[n])
            insides[b, 0] = mm(dscore_t[n], feat_q[n])
            insides[b, 1] = mm(weight_t[n], halfs[n])
            adjoints[b] = mm(feat_qt[n], grads[n])
            fks[b] = feat_k[n]
    map_grad_ref[...] = map_grad
    pair = jnp.where(lane < 2, 1.0, 0.0).astype(BF16)
    after = jnp.zeros((HEAD_DIM, 2 * HEAD_DIM), F32)
    for b in range(blocks - 1, -1, -1):
        halves_into(after, highs, lows, b)
        after = after + adjoints[b]
    for b in range(blocks):
        wide = jnp.concatenate([kv_ref[b, 1], pair], axis=1)
        feat_k = fks[b]
        part_ref[b, 0] = (mm_nt(wide, highs[b]) + mm_nt(wide, lows[b]) + insides[b, 0]).astype(PART)
        stacked = jnp.concatenate([highs[b, :, :HEAD_DIM], lows[b, :, :HEAD_DIM]], axis=0)
        part_ref[b, 1] = (mm(jnp.concatenate([feat_k, feat_k], axis=1), stacked) + insides[b, 1]).astype(PART)
    for store in stores:
        store.wait()


def outer(place_ref, kv_ref, map_ref, sums_ref, aq_ref, part_ref, out_ref, *refs):
    pieces, sem = refs[:-1], refs[-1]
    place = place_ref[0]
    copies = [pltpu.make_async_copy(aq_ref.at[0, place_ref[1] ^ s], piece.at[pl.ds(0, 2)], sem.at[s])
              for s, piece in enumerate(pieces)]
    for copy in copies:
        copy.start()
    after = jnp.zeros((HEAD_DIM, HEAD_DIM), F32)
    norms = []
    for z in range(sums_ref.shape[0]):
        part = jnp.where(z > place, sums_ref[z].astype(F32), 0.0)
        after = after + part[:HEAD_DIM]
        norms.append(part[HEAD_DIM:HEAD_DIM + 8])
    norms = jnp.concatenate(norms, axis=0).astype(BF16)
    first = jnp.where(lax.broadcasted_iota(jnp.int32, norms.shape, 1) == 0, 1.0, 0.0).astype(BF16)
    after = jnp.concatenate([after, mm_tn(norms, first)], axis=1)
    high, low = halves(after)
    stacked = jnp.concatenate([high[:, :HEAD_DIM], low[:, :HEAD_DIM]], axis=0)
    pair = jnp.where(lanes(BLOCK) == 0, 1.0, 0.0).astype(BF16)
    map_grad = jnp.zeros((HEAD_DIM, HEAD_DIM), F32)
    for group in groups_of(len(pieces)):
        at = [place_ref[1] ^ s for s in group]
        feat_k = [feature(mm(kv_ref[b, 0], map_ref[1])).astype(BF16) for b in at]
        wide = [jnp.concatenate([kv_ref[b, 1], pair], axis=1) for b in at]
        d_feat = [mm_nt(w, high) + mm_nt(w, low) + part_ref[b, 0].astype(F32) for b, w in zip(at, wide)]
        dpre = [(d * jnp.minimum(f.astype(F32), 1.0)).astype(BF16) for d, f in zip(d_feat, feat_k)]
        d_value = [mm(jnp.concatenate([f, f], axis=1), stacked) + part_ref[b, 1].astype(F32)
                   for b, f in zip(at, feat_k)]
        for n, s in enumerate(group):
            pieces[s][2] = mm_nt(dpre[n], map_ref[1]).astype(BF16)
            pieces[s][3] = d_value[n].astype(BF16)
            map_grad = map_grad + mm_tn(kv_ref[at[n], 0], dpre[n])
    out_ref[...] = map_grad
    for copy in copies:
        copy.wait()


def shape(*dims, dtype=BF16):
    return jax.ShapeDtypeStruct(dims, dtype)


def call(kernel, outs, operands, scratch=(), cycles=1, limit=32):
    return pl.pallas_call(
        kernel,
        out_shape=[s for _, s in outs],
        in_specs=[spec for spec, _ in operands],
        out_specs=[spec for spec, _ in outs],
        scratch_shapes=list(scratch),
        compiler_params=pltpu.CompilerParams(vmem_limit_bytes=limit * 1024 * 1024),
        cost_estimate=pl.CostEstimate(flops=cycles * 500_000_000, bytes_accessed=cycles * 2_000_000, transcendentals=0),
    )(*[v for _, v in operands])


def trade(pieces):
    count = len(pieces)
    return [pieces[0]] + [
        lax.ppermute(pieces[s], ROW, [(i, i ^ s) for i in range(count)]) for s in range(1, count)
    ]


def gather_maps(maps):
    z_size, y_size = lax.axis_size("z"), lax.axis_size("y")
    row = lax.axis_size(ROW)
    own, _, heads, cut = maps.shape
    maps = maps.transpose(2, 0, 1, 3).reshape(y_size, row, own * 2 * cut)
    maps = maps.transpose(1, 0, 2).reshape(1, heads, own * 2 * cut)
    return jnp.broadcast_to(maps, (z_size, heads, own * 2 * cut)).reshape(z_size * heads, -1)


def body(queries, keys, values, out_grad, feature_weights):
    z_size = lax.axis_size("z")
    row = lax.axis_size("x") * lax.axis_size("core")
    own, _, heads, cut = feature_weights.shape
    tokens = queries.shape[0] * lax.axis_size(CTX)
    place = jnp.stack([lax.axis_index("z"), lax.axis_index(ROW)]).astype(jnp.int32)
    scratch = pltpu.VMEM
    four = (4, BLOCK, HEAD_DIM)
    paired = (VMEM, shape(row, 2, BLOCK, HEAD_DIM))
    sums = (VMEM, shape(z_size, STATE_ROWS, HEAD_DIM))
    square = (VMEM, shape(HEAD_DIM, HEAD_DIM, dtype=F32))

    pieces = call(
        pack, [(ANY, shape(*four))] * row, [(ANY, v) for v in (keys, values, queries, out_grad)],
        [scratch((row, *four), BF16), DMA((row, 4)), DMA((row,))], limit=60)
    pieces = trade(pieces)
    maps = gather_maps(feature_weights)
    maps, pieces[1] = lax.optimization_barrier((maps, pieces[1]))
    maps = lax.all_to_all(maps, FINE, 0, 0, tiled=True)
    maps = maps.reshape(z_size * row, heads // row, own, 2, cut).transpose(3, 0, 2, 1, 4)
    maps = maps.reshape(2, HEAD_DIM, HEAD_DIM)
    kv, qd, state = call(
        key_state, [paired, paired, sums], [(SMEM, place), (VMEM, maps)] + [(VMEM, v) for v in pieces])
    state = lax.all_to_all(state, "z", 0, 0, tiled=True)
    halved = [scratch((row, HEAD_DIM, 2 * HEAD_DIM), BF16)] * 2
    total, prior = call(
        forward, [sums, (VMEM, shape(HEAD_DIM, 2 * HEAD_DIM, dtype=F32))],
        [(SMEM, place), (VMEM, kv), (VMEM, qd), (VMEM, maps), (VMEM, state)], halved, cycles=4)
    total = lax.all_to_all(total, "z", 0, 0, tiled=True)
    aq, part, map_grad_q = call(
        inner,
        [(ANY, shape(HELD, row, 2, BLOCK, HEAD_DIM)), (VMEM, shape(row, 2, BLOCK, HEAD_DIM, dtype=PART)), square],
        [(VMEM, kv), (VMEM, qd), (VMEM, maps), (VMEM, prior)],
        halved + [scratch((row, 2, BLOCK, HEAD_DIM), F32), scratch((row, HEAD_DIM, 2 * HEAD_DIM), F32),
                  scratch((row, BLOCK, HEAD_DIM), BF16), scratch((row, 2, BLOCK, HEAD_DIM), BF16), DMA((row,))],
        cycles=6)
    map_grad_k, *pieces = call(
        outer, [square] + [(VMEM, shape(*four))] * row,
        [(SMEM, place), (VMEM, kv), (VMEM, maps), (VMEM, total), (ANY, aq), (VMEM, part)],
        [DMA((row,))], cycles=3, limit=OUTER_LIMIT)
    pieces = trade(pieces)

    map_grad = jnp.stack((map_grad_q, map_grad_k)).reshape(2, z_size * row, own, heads // row, cut)
    map_grad = map_grad.transpose(1, 3, 2, 0, 4).reshape(z_size * heads, own * 2 * cut)
    map_grad, pieces[1] = lax.optimization_barrier((map_grad, pieces[1]))
    map_grad = lax.all_to_all(map_grad, FINE, 0, 0, tiled=True)
    map_grad = jnp.sum(map_grad.reshape(z_size, heads, own * 2 * cut), axis=0) / tokens
    map_grad = map_grad.reshape(row, heads // row, own, 2, cut).transpose(2, 3, 1, 0, 4)
    map_grad = map_grad.reshape(own, 2, heads, cut)
    attended, query_grad, key_grad, value_grad = call(
        unpack, [(ANY, shape(*queries.shape))] * 4, [(SMEM, place)] + [(VMEM, v) for v in pieces], [DMA((row, 4))])
    return attended, query_grad, key_grad, value_grad, map_grad


def solution(mesh):
    fine = Mesh(mesh.devices.reshape(8, 4, 2, 4), FINE)
    flat = P(CTX, "y")
    maps = P(CTX, None, None, "y")
    return jax.shard_map(
        body,
        mesh=fine,
        in_specs=(flat, flat, flat, flat, maps),
        out_specs=(flat, flat, flat, flat, maps),
        check_vma=False,
    )
```

```python
import jax
import jax.numpy as jnp
from jax import lax
from jax.experimental import pallas as pl
from jax.experimental.pallas import tpu as pltpu
from jax.sharding import Mesh
from jax.sharding import PartitionSpec as P

HEAD_DIM = 128
BLOCK = 256
F32 = jnp.float32
BF16 = jnp.bfloat16
ROW = ("x", "core")
CTX = ("z", "x", "core")
FINE = ("z", "x", "core", "y")
ANY = pl.BlockSpec(memory_space=pl.ANY)
VMEM = pl.BlockSpec(memory_space=pltpu.VMEM)
SMEM = pl.BlockSpec(memory_space=pltpu.SMEM)
DMA = pltpu.SemaphoreType.DMA
PART = BF16
STATE_ROWS = HEAD_DIM + 16
GROUP = 8
OUTER_LIMIT = 32
HELD = 40


def mm(a, b):
    return lax.dot_general(a, b, (((1,), (0,)), ((), ())), preferred_element_type=F32)


def mm_nt(a, b):
    return lax.dot_general(a, b, (((1,), (1,)), ((), ())), preferred_element_type=F32)


def mm_tn(a, b):
    return lax.dot_general(a, b, (((0,), (0,)), ((), ())), preferred_element_type=F32)


def feature(pre):
    return jnp.where(pre > 0, pre + 1.0, jnp.exp(jnp.minimum(pre, 0.0)))


def halves(value):
    high = value.astype(BF16)
    return high, (value - high.astype(F32)).astype(BF16)


def causal_mask():
    rows = lax.broadcasted_iota(jnp.int32, (BLOCK, BLOCK), 0)
    cols = lax.broadcasted_iota(jnp.int32, (BLOCK, BLOCK), 1)
    return rows >= cols


def lanes(rows):
    return lax.broadcasted_iota(jnp.int32, (rows, HEAD_DIM), 1)


def row_slope(grad, attended):
    return jnp.broadcast_to(-jnp.sum(grad * attended, axis=1, keepdims=True), grad.shape)


def norm_rows(column, centre):
    rows = column.T[:16]
    index = lax.broadcasted_iota(jnp.int32, (16, HEAD_DIM), 0)
    high = rows.astype(BF16).astype(F32)
    mid = (rows - high).astype(BF16).astype(F32)
    low = rows - high - mid
    parts = jnp.where(index == 0, high, jnp.where(index == 1, mid, jnp.where(index == 2, low, 0.0)))
    return jnp.where(index < 8, parts, jnp.broadcast_to(centre, (16, HEAD_DIM))).astype(BF16)


def turned(matrix):
    return matrix.astype(F32).T.astype(BF16)


def halves_into(value, high_ref, low_ref, b):
    high, low = halves(value)
    high_ref[b] = high
    low_ref[b] = low


def pack(*refs):
    me = lax.axis_index(ROW)
    ins, outs, (held, in_sem, out_sem) = refs[:4], refs[4:-3], refs[-3:]
    loads, stores = [], []
    for s in range(len(outs)):
        column = pl.ds(pl.multiple_of((me ^ s) * HEAD_DIM, HEAD_DIM), HEAD_DIM)
        for n, ref in enumerate(ins):
            loads.append(pltpu.make_async_copy(ref.at[:, column], held.at[s, n], in_sem.at[s, n]))
        stores.append(pltpu.make_async_copy(held.at[s], outs[s], out_sem.at[s]))
    for load in loads:
        load.start()
    for s, store in enumerate(stores):
        for load in loads[4 * s:4 * s + 4]:
            load.wait()
        store.start()
    for store in stores:
        store.wait()


def own_columns(me, outs, piece, sem):
    column = pl.ds(pl.multiple_of(me * HEAD_DIM, HEAD_DIM), HEAD_DIM)
    return [pltpu.make_async_copy(piece.at[n], ref.at[:, column], sem.at[n]) for n, ref in enumerate(outs)]


def unpack(place_ref, *refs):
    pieces, outs, sem = refs[4:-5], refs[-5:-1], refs[-1]
    copies = []
    for s, piece in enumerate(pieces, start=1):
        copies += own_columns(place_ref[1] ^ s, outs, piece, sem.at[s])
    for copy in copies:
        copy.start()
    for copy in copies:
        copy.wait()


def key_state(place_ref, map_ref, *refs):
    pieces, (kv_ref, qd_ref, out_ref) = refs[:-3], refs[-3:]
    blocks = len(pieces)
    me = place_ref[1]
    for s, piece in enumerate(pieces):
        kv_ref[me ^ s] = piece[:2]
        qd_ref[me ^ s] = piece[2:]
    key_map = turned(map_ref[1])
    total = jnp.zeros((HEAD_DIM, 2 * HEAD_DIM), F32)
    mean = jnp.zeros((1, HEAD_DIM), F32)
    feats = [feature(mm_nt(key_map, piece[0])).astype(BF16) for piece in pieces]
    for feat, piece in zip(feats, pieces):
        value = piece[1]
        mean = mean + jnp.sum(value.astype(F32), axis=0, keepdims=True)
        total = total + mm(feat, with_ones(value))
    centre = (mean * (1.0 / (blocks * BLOCK))).astype(BF16).astype(F32)
    column = total[:, HEAD_DIM:]
    state = (total[:, :HEAD_DIM] - column * centre).astype(BF16)
    norms = norm_rows(column, centre)
    for z in range(out_ref.shape[0]):
        out_ref[z, :HEAD_DIM] = state
        out_ref[z, HEAD_DIM:] = norms


def with_ones(value):
    return jnp.concatenate([value, jnp.ones((BLOCK, HEAD_DIM), BF16)], axis=1)


def prior_of(place, sums_ref):
    prior = jnp.zeros((HEAD_DIM, HEAD_DIM), F32)
    norms, centres = [], []
    for z in range(sums_ref.shape[0]):
        part = jnp.where(z < place, sums_ref[z].astype(F32), 0.0)
        prior = prior + part[:HEAD_DIM]
        norms.append(part[HEAD_DIM:HEAD_DIM + 8])
        centres.append(part[HEAD_DIM + 8:])
    centres = jnp.concatenate(centres, axis=0).astype(BF16)
    centres = jnp.concatenate([centres, jnp.ones_like(centres)], axis=1)
    prior = jnp.concatenate([prior, jnp.zeros_like(prior)], axis=1)
    return prior + mm_tn(jnp.concatenate(norms, axis=0).astype(BF16), centres)


def key_stage(prior, kv_ref, map_ref, highs, lows):
    blocks = kv_ref.shape[0]
    key_map = turned(map_ref[1])
    feats = [feature(mm_nt(key_map, kv_ref[b, 0])).astype(BF16) for b in range(blocks)]
    states = [mm(feats[b], with_ones(kv_ref[b, 1])) for b in range(blocks)]
    for b in range(blocks):
        halves_into(prior, highs, lows, b)
        prior = prior + states[b]
    return feats


def attend(group, kv_ref, qd_ref, feat_q, scores, highs, lows):
    weight = [s.astype(BF16) for s in scores]
    both = [mm(jnp.concatenate([f, f], axis=1), jnp.concatenate([highs[b], lows[b]], axis=0))
            for b, f in zip(group, feat_q)]
    inside = [mm(w, kv_ref[b, 1]) for b, w in zip(group, weight)]
    inverse = [1.0 / (p[:, HEAD_DIM:] + jnp.sum(s, axis=1, keepdims=True)) for p, s in zip(both, scores)]
    attended = [(p[:, :HEAD_DIM] + w) * i for p, w, i in zip(both, inside, inverse)]
    exact = [qd_ref[b, 1].astype(F32) * i for b, i in zip(group, inverse)]
    grad = [e.astype(BF16) for e in exact]
    across = [halves(row_slope(g.astype(F32), a)) for g, a in zip(grad, attended)]
    return attended, exact, grad, across


def groups_of(blocks):
    return [range(b, min(b + GROUP, blocks)) for b in range(0, blocks, GROUP)]


def forward(place_ref, kv_ref, qd_ref, map_ref, sums_ref, out_ref, prior_ref, highs, lows):
    blocks = kv_ref.shape[0]
    prior = prior_of(place_ref[0], sums_ref)
    prior_ref[...] = prior
    feats = key_stage(prior, kv_ref, map_ref, highs, lows)
    query_map = turned(map_ref[0])
    causal = causal_mask()
    lane = lanes(BLOCK)
    total = jnp.zeros((HEAD_DIM, 2 * HEAD_DIM), F32)
    centre = jnp.zeros((1, HEAD_DIM), F32)
    for group in groups_of(blocks):
        feat_q = [feature(mm(qd_ref[b, 0], map_ref[0])).astype(BF16) for b in group]
        feat_qt = [feature(mm_nt(query_map, qd_ref[b, 0])).astype(BF16) for b in group]
        scores = [jnp.where(causal, mm(f, feats[b]), 0.0) for b, f in zip(group, feat_q)]
        _, _, grads, across = attend(group, kv_ref, qd_ref, feat_q, scores, highs, lows)
        pairs = [jnp.where(lane == 0, a, jnp.where(lane == 1, r, jnp.zeros_like(r))) for a, r in across]
        for f, g, p in zip(feat_qt, grads, pairs):
            total = total + mm(f, jnp.concatenate([g, p], axis=1))
        for b in group:
            centre = centre + jnp.sum(kv_ref[b, 1].astype(F32), axis=0, keepdims=True)
    sent = total[:, :HEAD_DIM].astype(BF16)
    centre = (centre * (1.0 / (blocks * BLOCK))).astype(BF16).astype(F32)
    rest = jnp.sum((total[:, :HEAD_DIM] - sent.astype(F32)) * centre, axis=1, keepdims=True)
    column = jnp.sum(total[:, HEAD_DIM:], axis=1, keepdims=True) + rest
    norms = norm_rows(jnp.broadcast_to(column, (HEAD_DIM, HEAD_DIM)), jnp.zeros_like(centre))
    for z in range(out_ref.shape[0]):
        out_ref[z, :HEAD_DIM] = sent
        out_ref[z, HEAD_DIM:] = norms


def inner(kv_ref, qd_ref, map_ref, prior_ref, aq_ref, part_ref, map_grad_ref,
          highs, lows, insides, adjoints, fks, aq, sem):
    blocks = kv_ref.shape[0]
    feats = key_stage(prior_ref[...], kv_ref, map_ref, highs, lows)
    stores = [pltpu.make_async_copy(aq.at[b], aq_ref.at[0, b], sem.at[b]) for b in range(blocks)]
    query_map = turned(map_ref[0])
    causal = causal_mask()
    rows = lax.broadcasted_iota(jnp.int32, (BLOCK, BLOCK), 0)
    cols = lax.broadcasted_iota(jnp.int32, (BLOCK, BLOCK), 1)
    anti = rows <= cols
    lane = lanes(BLOCK)
    few = lanes(HEAD_DIM) < 2
    unit = jnp.where((lane == 2) | (lane == 3), 1.0, 0.0).astype(BF16)
    none = jnp.zeros((HEAD_DIM, HEAD_DIM), BF16)
    map_grad = jnp.zeros((HEAD_DIM, HEAD_DIM), F32)

    def narrow(part):
        return jnp.concatenate([part[:, :HEAD_DIM], jnp.where(few, part[:, HEAD_DIM:], none)], axis=1)

    for group in groups_of(blocks):
        feat_q = [feature(mm(qd_ref[b, 0], map_ref[0])).astype(BF16) for b in group]
        feat_qt = [feature(mm_nt(query_map, qd_ref[b, 0])).astype(BF16) for b in group]
        feat_k = [feature(mm(kv_ref[b, 0], map_ref[1])).astype(BF16) for b in group]
        scores = [jnp.where(causal, mm(f, feats[b]), 0.0) for b, f in zip(group, feat_q)]
        weight_t = [jnp.where(anti, mm(k, q), 0.0).astype(BF16) for k, q in zip(feat_k, feat_qt)]
        attended, exact, halfs, across = attend(group, kv_ref, qd_ref, feat_q, scores, highs, lows)
        within = [halves(row_slope(e, a)) for e, a in zip(exact, attended)]
        pairs = [jnp.where(lane == 0, a, jnp.where(lane == 1, r, jnp.zeros_like(r))) for a, r in across]
        pairs = [jnp.where(lane == 2, a, jnp.where(lane == 3, r, p)) for p, (a, r) in zip(pairs, within)]
        grads = [jnp.concatenate([g, p], axis=1) for g, p in zip(halfs, pairs)]
        values = [jnp.concatenate([kv_ref[b, 1], unit], axis=1) for b in group]
        dscore = [jnp.where(causal, mm_nt(g, v), 0.0).astype(BF16) for g, v in zip(grads, values)]
        dscore_t = [jnp.where(anti, mm_nt(v, g), 0.0).astype(BF16) for g, v in zip(grads, values)]
        d_feat = [mm_nt(g, narrow(highs[b])) + mm_nt(g, narrow(lows[b])) + mm(d, k)
                  for b, g, d, k in zip(group, grads, dscore, feat_k)]
        dpre = [(d * jnp.minimum(f.astype(F32), 1.0)).astype(BF16) for d, f in zip(d_feat, feat_q)]
        for n, b in enumerate(group):
            aq[b, 0] = attended[n].astype(BF16)
            aq[b, 1] = mm_nt(dpre[n], map_ref[0]).astype(BF16)
            stores[b].start()
            map_grad = map_grad + mm_tn(qd_ref[b, 0], dpre[n])
            insides[b, 0] = mm(dscore_t[n], feat_q[n])
            insides[b, 1] = mm(weight_t[n], halfs[n])
            adjoints[b] = mm(feat_qt[n], grads[n])
            fks[b] = feat_k[n]
    map_grad_ref[...] = map_grad
    pair = jnp.where(lane < 2, 1.0, 0.0).astype(BF16)
    after = jnp.zeros((HEAD_DIM, 2 * HEAD_DIM), F32)
    for b in range(blocks - 1, -1, -1):
        halves_into(after, highs, lows, b)
        after = after + adjoints[b]
    for b in range(blocks):
        wide = jnp.concatenate([kv_ref[b, 1], pair], axis=1)
        feat_k = fks[b]
        part_ref[b, 0] = (mm_nt(wide, highs[b]) + mm_nt(wide, lows[b]) + insides[b, 0]).astype(PART)
        stacked = jnp.concatenate([highs[b, :, :HEAD_DIM], lows[b, :, :HEAD_DIM]], axis=0)
        part_ref[b, 1] = (mm(jnp.concatenate([feat_k, feat_k], axis=1), stacked) + insides[b, 1]).astype(PART)
    for store in stores:
        store.wait()


def outer(place_ref, kv_ref, map_ref, sums_ref, aq_ref, part_ref, out_ref, *refs):
    outs, sent, (held, sem, own_sem) = refs[:4], refs[4:-3], refs[-3:]
    pieces = [held, *sent]
    place = place_ref[0]
    copies = [pltpu.make_async_copy(aq_ref.at[0, place_ref[1] ^ s], piece.at[pl.ds(0, 2)], sem.at[s])
              for s, piece in enumerate(pieces)]
    for copy in copies:
        copy.start()
    after = jnp.zeros((HEAD_DIM, HEAD_DIM), F32)
    norms = []
    for z in range(sums_ref.shape[0]):
        part = jnp.where(z > place, sums_ref[z].astype(F32), 0.0)
        after = after + part[:HEAD_DIM]
        norms.append(part[HEAD_DIM:HEAD_DIM + 8])
    norms = jnp.concatenate(norms, axis=0).astype(BF16)
    first = jnp.where(lax.broadcasted_iota(jnp.int32, norms.shape, 1) == 0, 1.0, 0.0).astype(BF16)
    after = jnp.concatenate([after, mm_tn(norms, first)], axis=1)
    high, low = halves(after)
    stacked = jnp.concatenate([high[:, :HEAD_DIM], low[:, :HEAD_DIM]], axis=0)
    pair = jnp.where(lanes(BLOCK) == 0, 1.0, 0.0).astype(BF16)
    map_grad = jnp.zeros((HEAD_DIM, HEAD_DIM), F32)
    for group in groups_of(len(pieces)):
        at = [place_ref[1] ^ s for s in group]
        feat_k = [feature(mm(kv_ref[b, 0], map_ref[1])).astype(BF16) for b in at]
        wide = [jnp.concatenate([kv_ref[b, 1], pair], axis=1) for b in at]
        d_feat = [mm_nt(w, high) + mm_nt(w, low) + part_ref[b, 0].astype(F32) for b, w in zip(at, wide)]
        dpre = [(d * jnp.minimum(f.astype(F32), 1.0)).astype(BF16) for d, f in zip(d_feat, feat_k)]
        d_value = [mm(jnp.concatenate([f, f], axis=1), stacked) + part_ref[b, 1].astype(F32)
                   for b, f in zip(at, feat_k)]
        for n, s in enumerate(group):
            pieces[s][2] = mm_nt(dpre[n], map_ref[1]).astype(BF16)
            pieces[s][3] = d_value[n].astype(BF16)
            map_grad = map_grad + mm_tn(kv_ref[at[n], 0], dpre[n])
    out_ref[...] = map_grad
    copies[0].wait()
    own = own_columns(place_ref[1], outs, held, own_sem)
    for copy in own:
        copy.start()
    for copy in copies[1:] + own:
        copy.wait()


def shape(*dims, dtype=BF16):
    return jax.ShapeDtypeStruct(dims, dtype)


def call(kernel, outs, operands, scratch=(), cycles=1, limit=32, aliases={}):
    return pl.pallas_call(
        kernel,
        out_shape=[s for _, s in outs],
        in_specs=[spec for spec, _ in operands],
        out_specs=[spec for spec, _ in outs],
        scratch_shapes=list(scratch),
        input_output_aliases=aliases,
        compiler_params=pltpu.CompilerParams(vmem_limit_bytes=limit * 1024 * 1024),
        cost_estimate=pl.CostEstimate(flops=cycles * 500_000_000, bytes_accessed=cycles * 2_000_000, transcendentals=0),
    )(*[v for _, v in operands])


def trade(pieces):
    count = len(pieces) + 1
    return [lax.ppermute(pieces[s - 1], ROW, [(i, i ^ s) for i in range(count)]) for s in range(1, count)]


def gather_maps(maps):
    z_size, y_size = lax.axis_size("z"), lax.axis_size("y")
    row = lax.axis_size(ROW)
    own, _, heads, cut = maps.shape
    maps = maps.transpose(2, 0, 1, 3).reshape(y_size, row, own * 2 * cut)
    maps = maps.transpose(1, 0, 2).reshape(1, heads, own * 2 * cut)
    return jnp.broadcast_to(maps, (z_size, heads, own * 2 * cut)).reshape(z_size * heads, -1)


def body(queries, keys, values, out_grad, feature_weights):
    z_size = lax.axis_size("z")
    row = lax.axis_size("x") * lax.axis_size("core")
    own, _, heads, cut = feature_weights.shape
    tokens = queries.shape[0] * lax.axis_size(CTX)
    place = jnp.stack([lax.axis_index("z"), lax.axis_index(ROW)]).astype(jnp.int32)
    scratch = pltpu.VMEM
    four = (4, BLOCK, HEAD_DIM)
    paired = (VMEM, shape(row, 2, BLOCK, HEAD_DIM))
    sums = (VMEM, shape(z_size, STATE_ROWS, HEAD_DIM))
    square = (VMEM, shape(HEAD_DIM, HEAD_DIM, dtype=F32))

    pieces = call(
        pack, [(ANY, shape(*four))] * row, [(ANY, v) for v in (keys, values, queries, out_grad)],
        [scratch((row, *four), BF16), DMA((row, 4)), DMA((row,))], limit=60)
    pieces = [pieces[0], *trade(pieces[1:])]
    maps = gather_maps(feature_weights)
    maps, pieces[1] = lax.optimization_barrier((maps, pieces[1]))
    maps = lax.all_to_all(maps, FINE, 0, 0, tiled=True)
    maps = maps.reshape(z_size * row, heads // row, own, 2, cut).transpose(3, 0, 2, 1, 4)
    maps = maps.reshape(2, HEAD_DIM, HEAD_DIM)
    kv, qd, state = call(
        key_state, [paired, paired, sums], [(SMEM, place), (VMEM, maps)] + [(VMEM, v) for v in pieces])
    state = lax.all_to_all(state, "z", 0, 0, tiled=True)
    halved = [scratch((row, HEAD_DIM, 2 * HEAD_DIM), BF16)] * 2
    total, prior = call(
        forward, [sums, (VMEM, shape(HEAD_DIM, 2 * HEAD_DIM, dtype=F32))],
        [(SMEM, place), (VMEM, kv), (VMEM, qd), (VMEM, maps), (VMEM, state)], halved, cycles=4)
    total = lax.all_to_all(total, "z", 0, 0, tiled=True)
    aq, part, map_grad_q = call(
        inner,
        [(ANY, shape(HELD, row, 2, BLOCK, HEAD_DIM)), (VMEM, shape(row, 2, BLOCK, HEAD_DIM, dtype=PART)), square],
        [(VMEM, kv), (VMEM, qd), (VMEM, maps), (VMEM, prior)],
        halved + [scratch((row, 2, BLOCK, HEAD_DIM), F32), scratch((row, HEAD_DIM, 2 * HEAD_DIM), F32),
                  scratch((row, BLOCK, HEAD_DIM), BF16), scratch((row, 2, BLOCK, HEAD_DIM), BF16), DMA((row,))],
        cycles=6)
    outs = [(ANY, shape(*queries.shape))] * 4
    map_grad_k, *pieces = call(
        outer, [square] + outs + [(VMEM, shape(*four))] * (row - 1),
        [(SMEM, place), (VMEM, kv), (VMEM, maps), (VMEM, total), (ANY, aq), (VMEM, part)],
        [scratch(four, BF16), DMA((row,)), DMA((4,))], cycles=3, limit=OUTER_LIMIT)
    owned, pieces = pieces[:4], trade(pieces[4:])

    map_grad = jnp.stack((map_grad_q, map_grad_k)).reshape(2, z_size * row, own, heads // row, cut)
    map_grad = map_grad.transpose(1, 3, 2, 0, 4).reshape(z_size * heads, own * 2 * cut)
    map_grad, pieces[0] = lax.optimization_barrier((map_grad, pieces[0]))
    map_grad = lax.all_to_all(map_grad, FINE, 0, 0, tiled=True)
    map_grad = jnp.sum(map_grad.reshape(z_size, heads, own * 2 * cut), axis=0) / tokens
    map_grad = map_grad.reshape(row, heads // row, own, 2, cut).transpose(2, 3, 1, 0, 4)
    map_grad = map_grad.reshape(own, 2, heads, cut)
    attended, query_grad, key_grad, value_grad = call(
        unpack, outs, [(SMEM, place)] + [(ANY, v) for v in owned] + [(VMEM, v) for v in pieces], [DMA((row, 4))],
        aliases={n + 1: n for n in range(4)})
    return attended, query_grad, key_grad, value_grad, map_grad


def solution(mesh):
    fine = Mesh(mesh.devices.reshape(8, 4, 2, 4), FINE)
    flat = P(CTX, "y")
    maps = P(CTX, None, None, "y")
    return jax.shard_map(
        body,
        mesh=fine,
        in_specs=(flat, flat, flat, flat, maps),
        out_specs=(flat, flat, flat, flat, maps),
        check_vma=False,
    )
```
